128 devices in a mesh: rep: 16 (over y, z_hi, core), grp: 8 (over z_lo, x).
Axes of the slice: x: 4, y: 4, z: 4 (z_hi: 2, z_lo: 2; z = z_hi * 2 + z_lo), core: 2. Of those that a mesh axis runs over, the one named last changes fastest.
Arguments:
- activations: bfloat16 [16384, 5120], P(('rep', 'grp')), may hold values from -20 to 20
- token_ids: int32 [16384], P('rep'), may hold values from 0 to 151935, as said below
- cotangent: bfloat16 [16384, 4096], P('rep', 'grp'), may hold values from -20 to 20
- inner_weight: bfloat16 [16, 32, 128, 5120], P('rep', 'grp'), may hold values from -6 to 6
- query_gain: float32 [128], replicated, may hold values from 0.1 to 1.9
- outer_weight: float32 [32, 128, 5120], P('grp', 'rep'), may hold values from -6 to 6
- momentum: float32 [32, 128, 5120], P('grp', 'rep'), may hold values from -6 to 6
- average_weight: float32 [32, 128, 5120], P('grp', 'rep'), may hold values from -6 to 6
Outputs:
- new_outer: float32 [32, 128, 5120], P('grp', 'rep')
- new_momentum: float32 [32, 128, 5120], P('grp', 'rep')
- new_average: float32 [32, 128, 5120], P('grp', 'rep')
The draws below stay inside these ranges and needn't reach their ends.
Inputs may be any that keep to these rules, and one draw needn't show every extreme that they name: `token_ids`: id 0 marks padding; padded positions form the tail of each aligned block of 128 tokens, at most half of it.
All inputs are finite; a program needn't handle non-finite values.
Results may differ from the reference program's by a relative error of at most 0.0015.
Values may be sent and summed in bfloat16 or wider, within the bound.
No kernel may reach another device: no remote copies, remote signals or barrier semaphores. Data moves between devices by JAX's collectives and lax.ppermute only.
A program may use at most 128 MiB of HBM per device.

```python
import math
import jax
import jax.numpy as jnp
from jax import lax

D = 5120
HD = 128
VOCAB = 151936
TOK_DEV = 128
ITERS = 5
HEADS = 32
TOK_REP = 1024
TOKENS = 16384
N_REP = 16


def scaled_field(key, row_total, column_total, low_scale, high_scale):
    first, second = jax.random.split(key, 2)
    column_scale = jnp.exp(jax.random.uniform(second, (column_total,), jnp.float32, math.log(low_scale), math.log(high_scale)))
    field_values = jax.random.normal(first, (row_total, column_total), jnp.float32) * column_scale
    return jnp.clip(field_values, -20.0, 20.0)


def draw_activations(key, part):
    key = jax.random.fold_in(key, 11)
    return scaled_field(key, TOKENS, D, 0.3, 3.0).astype(jnp.bfloat16)


def draw_cotangent(key, part):
    key = jax.random.fold_in(key, 23)
    return scaled_field(key, TOKENS, HEADS * HD, 0.3, 3.0).astype(jnp.bfloat16)


def draw_token_ids(key, part):
    key = jax.random.fold_in(key, 37)
    first, second = jax.random.split(key)
    block_count = TOKENS // TOK_DEV
    id_values = jax.random.randint(first, (block_count, TOK_DEV), 1, VOCAB)
    kept_length = jax.random.randint(second, (block_count, 1), TOK_DEV // 2, TOK_DEV + 1)
    position = jnp.arange(TOK_DEV)[None, :]
    return jnp.where(position < kept_length, id_values, 0).reshape(TOKENS).astype(jnp.int32)


def strengthened(entries, key, source, target, parts, factor):
    owner, partner = [(jnp.arange(entries.shape[dim]) // (entries.shape[dim] // parts)).reshape([-1 if axis == dim else 1 for axis in range(entries.ndim)]) for dim in (source, target)]
    chosen = jax.random.permutation(key, parts)[partner]
    strong = (owner == chosen) | (owner == (partner + parts // 2) % parts)
    return jnp.where(strong, factor * entries, entries)


def level_of(stream_key, shape, cuts, low, top_value):
    gain, own = 1.0, jax.random.fold_in(stream_key, 6)
    for dim, shards_of in cuts:
        steps = jnp.exp(jax.random.uniform(jax.random.fold_in(own, dim), (shards_of,), jnp.float32, low / len(cuts), top_value / len(cuts)))
        gain = gain * jnp.repeat(steps, shape[dim] // shards_of).reshape([-1 if axis == dim else 1 for axis in range(len(shape))])
    return gain


def noise(own_key, extent, deviation, reach, cuts=(), held_as=jnp.bfloat16):
    drawn = jax.random.normal(own_key, extent, jnp.float32) * deviation
    if len(cuts) > 0:
        drawn = level_of(own_key, extent, cuts, -0.22, 0.18) * drawn
    return jnp.clip(drawn, min=-reach, max=reach).astype(held_as)


def noise_with(own_key, extent, width, reach, cuts, heavy, kind=jnp.bfloat16):
    drawn = width * jax.random.normal(own_key, extent, jnp.float32)
    if cuts:
        drawn = drawn * level_of(own_key, extent, cuts, -0.22, 0.18)
    return jnp.clip(strengthened(drawn, jax.random.fold_in(own_key, 3), *heavy), -reach, reach).astype(kind)


def setup_inputs(seed: int = 0) -> dict:
    streams_of = jax.random.split(jax.random.key(seed), 9)
    return {
        "activations": draw_activations(jax.random.fold_in(streams_of[8], 71), 0),
        "token_ids": draw_token_ids(jax.random.fold_in(streams_of[8], 71), 0),
        "cotangent": draw_cotangent(jax.random.fold_in(streams_of[8], 71), 0),
        "inner_weight": noise_with(streams_of[3], (N_REP, HEADS, HD, D), 1.0, 6.0, ((0, 16), (1, 8)), (0, 2, 16, 2.0)),
        "query_gain": jnp.clip(1.0 + 0.18 * jax.random.normal(streams_of[4], (HD,), jnp.float32), 0.1, 1.9),
        "outer_weight": noise(streams_of[5], (HEADS, HD, D), 1.0, 6.0, ((0, 8), (1, 16)), jnp.float32),
        "momentum": noise(streams_of[6], (HEADS, HD, D), 1.0, 6.0, ((0, 8), (1, 16)), jnp.float32),
        "average_weight": noise(streams_of[7], (HEADS, HD, D), 1.0, 6.0, ((0, 8), (1, 16)), jnp.float32),
    }


COEF_A = 3.4445
COEF_B = -4.775
COEF_C = 2.0315

def norm_backward(queries, upstream, query_gain, live_rows):
    mean_square = lax.optimization_barrier(jnp.mean(queries * queries, axis=-1, keepdims=True)) + 1e-06
    inverse = lax.rsqrt(mean_square)
    normed = queries * inverse
    scaled = query_gain * upstream.astype(jnp.float32)
    projection = lax.optimization_barrier(jnp.mean(normed * scaled, axis=-1, keepdims=True))
    return (live_rows[:, None, None] * (scaled - normed * projection) * inverse).astype(jnp.bfloat16)

def orthogonalize(gradient):
    frobenius = jnp.sqrt(lax.optimization_barrier(jnp.sum(gradient * gradient, axis=(1, 2), keepdims=True)))
    iterate = gradient / (frobenius + 1e-07)
    for number in range(ITERS):
        gram_matrix = jnp.einsum('hik,hjk->hij', iterate, iterate, precision=lax.Precision.HIGHEST)
        squared = jnp.einsum('hij,hjk->hik', gram_matrix, gram_matrix, precision=lax.Precision.HIGHEST)
        polynomial = COEF_B * gram_matrix + COEF_C * squared
        applied = jnp.einsum('hij,hjk->hik', polynomial, iterate, precision=lax.Precision.HIGHEST)
        iterate = COEF_A * iterate + applied
    return iterate

def renew_weights(gradient, weights):
    orthogonal = orthogonalize(gradient)
    renewed = (weights.astype(jnp.float32) - 0.2 * math.sqrt(D) * orthogonal).astype(jnp.bfloat16)
    renewed = lax.optimization_barrier(renewed)
    return renewed.astype(jnp.float32)

def reference(activations, token_ids, cotangent, inner_weight, query_gain, outer_weight, momentum, average_weight):
    act_blocks = activations.reshape(N_REP, TOK_REP, D)
    id_blocks = token_ids.reshape(N_REP, TOK_REP)
    cot_blocks = cotangent.reshape(N_REP, TOK_REP, HEADS, HD)

    def replica_step(summed, pieces):
        token_block, id_block, upstream, weights = pieces
        flat_weight = weights.reshape(HEADS * HD, D)
        queries = jnp.dot(token_block, flat_weight.T, preferred_element_type=jnp.float32)
        live_rows = (id_block != 0).astype(jnp.float32)
        query_grad = norm_backward(queries.reshape(TOK_REP, HEADS, HD), upstream, query_gain, live_rows)
        query_grad = query_grad.reshape(TOK_REP, HEADS * HD)
        gradient = jnp.dot(query_grad.T, token_block, preferred_element_type=jnp.float32).reshape(HEADS, HD, D)
        return (summed + renew_weights(gradient, weights), None)
    start_sum = jnp.zeros((HEADS, HD, D), jnp.float32)
    summed, unused = lax.scan(replica_step, start_sum, (act_blocks, id_blocks, cot_blocks, inner_weight))
    mean_weight = summed / N_REP
    pseudo = outer_weight - mean_weight
    new_momentum = 0.9 * momentum + pseudo
    new_outer = outer_weight - 0.7 * (pseudo + 0.9 * new_momentum)
    new_average = 0.9 * average_weight + 0.1 * new_outer
    return (new_outer, new_momentum, new_average)
```

```python
import math

import jax
import jax.numpy as jnp
from jax import lax
from jax.sharding import PartitionSpec as P

ITERS = 5
COEF_A = 3.4445
COEF_B = -4.775
COEF_C = 2.0315

RING = 4
BLOCK = 128
ROWS_B = 48
ROWS_A = BLOCK - ROWS_B


def along_x(array, step):
    pairs = [(z * RING + x, z * RING + (x + step) % RING) for z in range(2) for x in range(RING)]
    return lax.ppermute(array, "grp", pairs)


def across_z(array):
    return lax.ppermute(array, "grp", [(g, (g + RING) % (2 * RING)) for g in range(2 * RING)])


def to_other_core(array):
    return lax.ppermute(array, "rep", [(r, r ^ 1) for r in range(16)])


def to_chip(array, step_y, step_z):
    pairs = []
    for y in range(4):
        for z in range(2):
            for core in range(2):
                source = (y * 2 + z) * 2 + core
                target = (((y + step_y) % 4) * 2 + (z + step_z) % 2) * 2 + core
                pairs.append((source, target))
    return lax.ppermute(array, "rep", pairs)


def query_gradient(tokens, flat_weight, upstream, query_gain, live_rows, head_count):
    rows = tokens.shape[0]
    queries = lax.dot_general(
        tokens, flat_weight, (((1,), (1,)), ((), ())), preferred_element_type=jnp.float32
    ).reshape(rows, head_count, -1)
    inverse = lax.rsqrt(jnp.mean(queries * queries, axis=-1, keepdims=True) + 1e-06)
    normed = queries * inverse
    scaled = query_gain * upstream.reshape(rows, head_count, -1).astype(jnp.float32)
    projection = jnp.mean(normed * scaled, axis=-1, keepdims=True)
    result = live_rows[:, None, None] * (scaled - normed * projection) * inverse
    return result.astype(jnp.bfloat16).reshape(rows, -1)


def weight_gradient(query_grad, tokens):
    return lax.dot_general(
        query_grad, tokens, (((0,), (0,)), ((), ())), preferred_element_type=jnp.float32
    )


def renew_weights(gradient, weights):
    head_size, model_width = weights.shape[1:]
    full = lax.Precision.HIGHEST
    gram = jnp.einsum("hik,hjk->hij", gradient, gradient, precision=full)
    square_sum = jnp.trace(gram, axis1=1, axis2=2)
    scale = 1.0 / (jnp.sqrt(square_sum) + 1e-07)
    gram = gram * (scale * scale)[:, None, None]
    eye = jnp.eye(head_size, dtype=jnp.float32)
    total = None
    for number in range(ITERS):
        squared = jnp.einsum("hij,hjk->hik", gram, gram, precision=full)
        step = COEF_A * eye + COEF_B * gram + COEF_C * squared
        total = step if total is None else jnp.einsum("hij,hjk->hik", step, total, precision=full)
        if number < ITERS - 1:
            half = jnp.einsum("hij,hjk->hik", step, gram, precision=full)
            gram = jnp.einsum("hij,hjk->hik", half, step, precision=full)
    total = total * (0.2 * math.sqrt(model_width) * scale)[:, None, None]
    change = jnp.einsum("hij,hjk->hik", total, gradient, precision=full)
    return (weights.astype(jnp.float32) - change).astype(jnp.bfloat16)


def shards(
    activations,
    token_ids,
    cotangent,
    inner_weight,
    query_gain,
    outer_weight,
    momentum,
    average_weight,
):
    weights = inner_weight[0]
    head_count, head_size, model_width = weights.shape
    flat_weight = weights.reshape(head_count * head_size, model_width)

    place = lax.axis_index("grp")
    place_z, place_x = place // RING, place % RING
    order = []
    for step_z in range(2):
        for step_x in (0, -1, 1, 2):
            order.append(((place_z + step_z) % 2) * RING + (place_x + step_x) % RING)
    order = jnp.stack(order)
    live = (token_ids != 0).astype(jnp.float32).reshape(2 * RING, BLOCK)[order].reshape(-1)
    upstream = cotangent.reshape(2 * RING, BLOCK, -1)[order].reshape(2 * RING * BLOCK, -1)

    own_a, own_b = activations[:ROWS_A], activations[ROWS_A:]
    left_b, right_b = along_x(own_b, 1), along_x(own_b, -1)
    left_a, right_a = along_x(own_a, 1), along_x(own_a, -1)
    over_a = across_z(own_a)
    over_b = across_z(own_b)
    far_b0, far_b1 = along_x(left_b[:32], 1), along_x(right_b[32:], -1)
    over_left_b, over_right_b = across_z(left_b), across_z(right_b)
    over_left_a, over_right_a = along_x(over_a, 1), along_x(over_a, -1)
    far_a0, far_a1 = along_x(left_a[:32], 1), along_x(right_a[32:], -1)
    far_b = jnp.concatenate([far_b0, far_b1])
    over_far_b = across_z(far_b)
    over_far_a0 = along_x(over_left_a[:48], 1)
    over_far_a1 = along_x(over_right_a[48:], -1)

    def both(first, second):
        return jnp.concatenate([first, second])

    early = jnp.concatenate(
        [activations, left_a, left_b, right_a, right_b, far_a0, far_a1, far_b, over_a, over_b]
    )
    early_rows = early.shape[0]
    early_grad = query_gradient(
        early, flat_weight, upstream[:early_rows], query_gain, live[:early_rows], head_count
    )
    early_sum = weight_gradient(early_grad, early)
    late = jnp.concatenate(
        [over_left_a, over_left_b, over_right_a, over_right_b, over_far_a0, over_far_a1, over_far_b]
    )
    late_grad = query_gradient(
        late, flat_weight, upstream[early_rows:], query_gain, live[early_rows:], head_count
    )
    gradient = early_sum + weight_gradient(late_grad, late)
    gradient = gradient.reshape(head_count, head_size, model_width)

    renewed = renew_weights(gradient, weights)

    spot = lax.axis_index("rep")
    spot_y, spot_z, core = spot // 4, (spot // 2) % 2, spot % 2
    share = outer_weight.shape[1]
    pieces = renewed.reshape(head_count, 4, 2, 2, share, model_width)

    def piece(step_y, step_z, of_core):
        start = (0, (spot_y + step_y) % 4, (spot_z + step_z) % 2, of_core, 0, 0)
        taken = lax.dynamic_slice(pieces, start, (head_count, 1, 1, 1, share, model_width))
        return taken.reshape(head_count, share, model_width)

    steps = [(2, 1), (2, 0), (1, 1), (3, 1), (1, 0), (3, 0), (0, 1), (0, 0)]
    theirs = to_other_core(jnp.stack([piece(y, z, 1 - core) for y, z in steps]))
    arrived = []
    for number, (step_y, step_z) in enumerate(steps):
        pair = piece(step_y, step_z, core).astype(jnp.float32) + theirs[number].astype(jnp.float32)
        if (step_y, step_z) != (0, 0):
            pair = to_chip(pair.astype(jnp.bfloat16), step_y, step_z).astype(jnp.float32)
        arrived.append(pair)
    summed = sum(arrived)

    mean_weight = summed / lax.axis_size("rep")
    pseudo = outer_weight - mean_weight
    new_momentum = 0.9 * momentum + pseudo
    new_outer = outer_weight - 0.7 * (pseudo + 0.9 * new_momentum)
    new_average = 0.9 * average_weight + 0.1 * new_outer
    return (new_outer, new_momentum, new_average)


def solution(mesh):
    placed = (
        P(("rep", "grp"), None),
        P("rep"),
        P("rep", "grp"),
        P("rep", "grp", None, None),
        P(),
        P("grp", "rep", None),
        P("grp", "rep", None),
        P("grp", "rep", None),
    )
    return jax.shard_map(
        shards,
        mesh=mesh,
        in_specs=placed,
        out_specs=(P("grp", "rep", None), P("grp", "rep", None), P("grp", "rep", None)),
        check_vma=False,
    )
```

```python
import functools
import math

import jax
import jax.numpy as jnp
from jax import lax
from jax.experimental import pallas as pl
from jax.experimental.pallas import tpu as pltpu
from jax.sharding import PartitionSpec as P

ITERS = 5
COEF_A = 3.4445
COEF_B = -4.775
COEF_C = 2.0315

RING = 4
BLOCK = 128
ROWS_A = 80
FAR, FAR_A = 64, 48
TILE = 640
EARLY_VMEM, LATE_VMEM, RENEW_VMEM = 18, 12, 26


def along_x(array, step):
    pairs = [(z * RING + x, z * RING + (x + step) % RING) for z in range(2) for x in range(RING)]
    return lax.ppermute(array, "grp", pairs)


def across_z(array):
    return lax.ppermute(array, "grp", [(g, (g + RING) % (2 * RING)) for g in range(2 * RING)])


def to_other_core(array):
    return lax.ppermute(array, "rep", [(r, r ^ 1) for r in range(16)])


def to_chip(array, step_y, step_z):
    pairs = []
    for y in range(4):
        for z in range(2):
            for core in range(2):
                source = (y * 2 + z) * 2 + core
                target = (((y + step_y) % 4) * 2 + (z + step_z) % 2) * 2 + core
                pairs.append((source, target))
    return lax.ppermute(array, "rep", pairs)


def contract(left, right, left_dim, right_dim):
    return lax.dot_general(
        left, right, (((left_dim,), (right_dim,)), ((), ())), preferred_element_type=jnp.float32
    )


def halves(value):
    high = value.astype(jnp.bfloat16)
    return high, (value - high.astype(jnp.float32)).astype(jnp.bfloat16)


def product(left, right):
    high, low = left
    right_high, right_low = right
    wide = contract(
        jnp.concatenate([high, low], 1), jnp.concatenate([right_high, right_high], 0), 1, 0
    )
    return wide + contract(high, right_low, 1, 0)


def orthogonal_factors(grams, width):
    size = grams[0].shape[0]
    eye = (
        lax.broadcasted_iota(jnp.int32, (size, size), 0)
        == lax.broadcasted_iota(jnp.int32, (size, size), 1)
    ).astype(jnp.float32)
    scales, current = [], []
    for gram in grams:
        square_sum = jnp.sum(gram * eye, keepdims=True)
        scale = 1.0 / (jnp.sqrt(square_sum) + 1e-07)
        scales.append(scale)
        current.append(gram * scale * scale)
    totals = None
    for number in range(ITERS):
        split = [halves(gram) for gram in current]
        squares = [product(gram, gram) for gram in split]
        steps = [
            COEF_A * eye + COEF_B * gram + COEF_C * square for gram, square in zip(current, squares)
        ]
        step_split = [halves(step) for step in steps]
        if totals is None:
            totals_next = steps
        else:
            total_split = [halves(total) for total in totals]
            totals_next = [product(s, t) for s, t in zip(step_split, total_split)]
        if number < ITERS - 1:
            half = [halves(product(s, g)) for s, g in zip(step_split, split)]
            current = [product(h, s) for h, s in zip(half, step_split)]
        totals = totals_next
    factor = 0.2 * math.sqrt(width)
    return [total * (scale * factor) for total, scale in zip(totals, scales)]


class Copies:
    def __init__(self, sems):
        self.sems, self.count = sems, 0

    def start(self, source, target):
        copy = pltpu.make_async_copy(source, target, self.sems.at[self.count])
        copy.start()
        self.count += 1
        return copy


def start_tokens(copies, pieces, spans, tokens, offset=0):
    started = []
    for piece, (begin, count) in zip(pieces, spans):
        target = tokens.at[pl.ds(offset, count)]
        started.append(copies.start(piece.at[pl.ds(begin, count)], target))
        offset += count
    return started


def start_upstream(copies, place_ref, first_block, upstream_ref, upstream):
    started = []
    for block in range(upstream.shape[0] // BLOCK):
        begin = pl.multiple_of(place_ref[first_block + block] * BLOCK, BLOCK)
        target = upstream.at[pl.ds(block * BLOCK, BLOCK)]
        started.append(copies.start(upstream_ref.at[pl.ds(begin, BLOCK)], target))
    return started


def wait_all(copies):
    for copy in copies:
        copy.wait()


def head_gradient(queries, upstream, gain):
    inverse = lax.rsqrt(jnp.mean(queries * queries, axis=0, keepdims=True) + 1e-06)
    normed = queries * inverse
    scaled = gain * upstream
    projection = jnp.mean(normed * scaled, axis=0, keepdims=True)
    return (scaled - normed * projection) * inverse


def rotated_gradient(
    place_ref, first_block, gain_ref, ids_ref, tokens, weight, upstream, turned, rotated, base, ready
):
    rows = upstream.shape[0]
    size = gain_ref.shape[0]
    heads = weight.shape[0] // size
    for block in range(rows // BLOCK):
        span = slice(block * BLOCK, (block + 1) * BLOCK)
        for head in range(heads):
            columns = slice(head * size, (head + 1) * size)
            turned[columns, span] = upstream[span, columns].astype(jnp.float32).T
    live = []
    for block in range(rows // BLOCK):
        ids = ids_ref[pl.ds(place_ref[first_block + block], 1), :]
        live.append((ids != 0).astype(jnp.float32))
    gain = gain_ref[...]
    wait_all(ready)
    for block in range(rows // BLOCK):
        span = pl.ds(base + block * BLOCK, BLOCK)
        queries = contract(weight[...], tokens[span, :], 1, 1)
        for head in range(heads):
            columns = slice(head * size, (head + 1) * size)
            there = slice(block * BLOCK, (block + 1) * BLOCK)
            grad = head_gradient(queries[columns], turned[columns, there], gain)
            rotated[columns, span] = (grad * live[block]).astype(jnp.bfloat16)


def early_kernel(first_block, spans, *refs):
    count = len(spans)
    place_ref, gain_ref, ids_ref, upstream_ref, weight = refs[:5]
    pieces, refs = refs[5 : 5 + count], refs[5 + count :]
    out_ref, zero_ref, tokens, upstream, turned, rotated, sems = refs
    copies = Copies(sems)
    needed = start_upstream(copies, place_ref, first_block, upstream_ref, upstream)
    ready = start_tokens(copies, pieces, spans, tokens)
    zero_ref[0] = 0
    wait_all(needed)
    rotated_gradient(
        place_ref, first_block, gain_ref, ids_ref, tokens, weight, upstream, turned, rotated, 0, ready
    )

    @pl.loop(0, out_ref.shape[1] // TILE)
    def _(tile):
        columns = pl.ds(pl.multiple_of(tile * TILE, TILE), TILE)
        out_ref[:, columns] = contract(rotated[...], tokens[:, columns], 1, 0)


def late_kernel(first_block, spans, *refs):
    count = len(spans)
    place_ref, gain_ref, ids_ref, upstream_ref, weight = refs[:5]
    pieces, refs = refs[5 : 5 + count], refs[5 + count :]
    out_ref, tokens, upstream, turned, sems = refs
    copies = Copies(sems)
    needed = start_upstream(copies, place_ref, first_block, upstream_ref, upstream)
    ready = start_tokens(copies, pieces, spans, tokens)
    wait_all(needed)
    rotated_gradient(
        place_ref, first_block, gain_ref, ids_ref, tokens, weight, upstream, turned, out_ref, 0, ready
    )


def renew_kernel(first_block, late_spans, spans, *refs):
    late_count, count = len(late_spans), len(spans)
    place_ref, gain_ref, ids_ref, upstream_ref, weight, before_ref, late_ref = refs[:7]
    late, refs = refs[7 : 7 + late_count], refs[7 + late_count :]
    pieces, (mine_ref, theirs_ref) = refs[:count], refs[count : count + 2]
    tokens, upstream, turned, rotated, split, factors, sems = refs[count + 2 :]
    all_rows, width = weight.shape
    size = gain_ref.shape[0]
    heads = all_rows // size
    tiles = width // TILE
    rows = upstream.shape[0]
    late_rows = tokens.shape[0] - rows
    copies = Copies(sems)
    needed = start_upstream(copies, place_ref, first_block, upstream_ref, upstream)
    ready = start_tokens(copies, pieces, spans, tokens, late_rows)
    others = start_tokens(copies, late, late_spans, tokens)
    rotated[:, :late_rows] = late_ref[...]
    wait_all(needed)
    rotated_gradient(
        place_ref, first_block, gain_ref, ids_ref, tokens, weight, upstream, turned, rotated,
        late_rows, ready,
    )
    wait_all(others)

    @pl.loop(0, tiles)
    def _(tile):
        columns = pl.ds(pl.multiple_of(tile * TILE, TILE), TILE)
        part = contract(rotated[...], tokens[:, columns], 1, 0) + before_ref[:, columns]
        high, low = halves(part)
        for head in range(heads):
            span = slice(head * size, (head + 1) * size)
            split[head, :size, columns] = high[span]
            split[head, size:, columns] = low[span]

    grams = []
    for head in range(heads):
        both = split[head]
        whole = contract(both, both, 1, 1)
        grams.append(
            whole[:size, :size] + whole[:size, size:] + whole[size:, :size] + whole[size:, size:]
        )
    for head, factor in enumerate(orthogonal_factors(grams, width)):
        high, low = halves(factor)
        factors[head, :size, :size] = high
        factors[head, :size, size:] = high
        factors[head, size:, :size] = low
        factors[head, size:, size:] = jnp.zeros_like(low)

    core_is_zero = place_ref[10] == 0
    indices = []
    for chip in range(8):
        step_y = lax.rem(chip // 2 - place_ref[8] + 4, 4)
        step_z = lax.rem(chip % 2 - place_ref[9] + 2, 2)
        indices.append(step_y * 2 + step_z)

    @pl.loop(0, tiles)
    def _(tile):
        columns = pl.ds(pl.multiple_of(tile * TILE, TILE), TILE)
        for pair in range(heads // 2):
            renewed = []
            for head in (2 * pair, 2 * pair + 1):
                both = contract(factors[head], split[head, :, columns], 1, 0)
                change = both[:size] + both[size:]
                old = weight[head * size : (head + 1) * size, columns].astype(jnp.float32)
                renewed.append(old - change)
            span = pl.ds(pair * 16, 16)
            for chip, index in enumerate(indices):
                parts = []
                for core in range(2):
                    begin = (chip * 2 + core) * 8
                    parts.append(
                        jnp.concatenate([value[begin : begin + 8] for value in renewed], 0)
                    )
                mine = jnp.where(core_is_zero, parts[0], parts[1])
                theirs = jnp.where(core_is_zero, parts[1], parts[0])
                mine_ref[index, span, columns] = mine.astype(jnp.bfloat16)
                theirs_ref[index, span, columns] = theirs.astype(jnp.bfloat16)


ANYWHERE = pl.BlockSpec(memory_space=pl.ANY)
INSIDE = pl.BlockSpec(memory_space=pltpu.VMEM)
SCALARS = pl.BlockSpec(memory_space=pltpu.SMEM)


def call(kernel, out_shape, in_specs, out_specs, scratch, flops, moved, vmem, operands):
    return pl.pallas_call(
        kernel,
        out_shape=out_shape,
        in_specs=in_specs,
        out_specs=out_specs,
        scratch_shapes=scratch,
        compiler_params=pltpu.CompilerParams(vmem_limit_bytes=vmem * 1024 * 1024),
        cost_estimate=pl.CostEstimate(flops=flops, bytes_accessed=moved, transcendentals=0),
    )(*operands)


def scratch_of(common, rows):
    all_rows, width = common[-1].shape
    return [
        pltpu.VMEM((rows, all_rows), jnp.bfloat16),
        pltpu.VMEM((all_rows, rows), jnp.float32),
    ]


def arrays_of(pieces):
    return [piece[0] if isinstance(piece, tuple) else piece for piece in pieces]


def spans_of(pieces):
    return [piece[1:] if isinstance(piece, tuple) else (0, piece.shape[0]) for piece in pieces]


def rows_of(pieces):
    return sum(count for _, count in spans_of(pieces))


COMMON_SPECS = [SCALARS, INSIDE, INSIDE, ANYWHERE, INSIDE]


def early_call(common, first_block, pieces):
    all_rows, width = common[-1].shape
    rows = rows_of(pieces)
    return call(
        functools.partial(early_kernel, first_block, spans_of(pieces)),
        (
            jax.ShapeDtypeStruct((all_rows, width), jnp.float32),
            jax.ShapeDtypeStruct((1,), jnp.int32),
        ),
        COMMON_SPECS + [ANYWHERE] * len(pieces),
        (INSIDE, SCALARS),
        [pltpu.VMEM((rows, width), jnp.bfloat16)]
        + scratch_of(common, rows)
        + [
            pltpu.VMEM((all_rows, rows), jnp.bfloat16),
            pltpu.SemaphoreType.DMA((len(pieces) + rows // BLOCK,)),
        ],
        4 * rows * all_rows * width,
        (6 * all_rows + 2 * rows) * width,
        EARLY_VMEM,
        [*common, *arrays_of(pieces)],
    )


def late_call(common, first_block, pieces):
    all_rows, width = common[-1].shape
    rows = rows_of(pieces)
    return call(
        functools.partial(late_kernel, first_block, spans_of(pieces)),
        jax.ShapeDtypeStruct((all_rows, rows), jnp.bfloat16),
        COMMON_SPECS + [ANYWHERE] * len(pieces),
        INSIDE,
        [pltpu.VMEM((rows, width), jnp.bfloat16)]
        + scratch_of(common, rows)
        + [pltpu.SemaphoreType.DMA((len(pieces) + rows // BLOCK,))],
        2 * rows * all_rows * width,
        2 * (rows + all_rows) * width,
        LATE_VMEM,
        [*common, *arrays_of(pieces)],
    )


def renew_call(common, first_block, before, late_rotated, late, pieces):
    all_rows, width = common[-1].shape
    size = common[1].shape[0]
    heads = all_rows // size
    rows = rows_of(pieces)
    total = rows + rows_of(late)
    shape = jax.ShapeDtypeStruct((8, all_rows // 16, width), jnp.bfloat16)
    return call(
        functools.partial(renew_kernel, first_block, spans_of(late), spans_of(pieces)),
        (shape, shape),
        COMMON_SPECS + [INSIDE, INSIDE] + [ANYWHERE] * (len(late) + len(pieces)),
        (INSIDE, INSIDE),
        [pltpu.VMEM((total, width), jnp.bfloat16)]
        + scratch_of(common, rows)
        + [
            pltpu.VMEM((all_rows, total), jnp.bfloat16),
            pltpu.VMEM((heads, 2 * size, width), jnp.bfloat16),
            pltpu.VMEM((heads, 2 * size, 2 * size), jnp.bfloat16),
            pltpu.SemaphoreType.DMA((len(late) + len(pieces) + rows // BLOCK,)),
        ],
        (4 * rows + 16 * size) * all_rows * width,
        8 * all_rows * width,
        RENEW_VMEM,
        [*common, before, late_rotated, *arrays_of(late), *arrays_of(pieces)],
    )


def shards(
    activations,
    token_ids,
    cotangent,
    inner_weight,
    query_gain,
    outer_weight,
    momentum,
    average_weight,
):
    weights = inner_weight[0]
    head_count, head_size, model_width = weights.shape
    flat_weight = weights.reshape(head_count * head_size, model_width)

    place = lax.axis_index("grp")
    spot = lax.axis_index("rep")
    numbers = []
    for step_z, step_x in ((0, 0), (0, -1), (0, 1), (1, 0), (0, 2), (1, -1), (1, 1), (1, 2)):
        numbers.append(((place // RING + step_z) % 2) * RING + (place + step_x) % RING)
    numbers += [spot // 4, (spot // 2) % 2, spot % 2]
    common = (
        jnp.stack(numbers).astype(jnp.int32),
        query_gain[:, None],
        token_ids.reshape(2 * RING, BLOCK),
        cotangent,
        flat_weight,
    )

    left, right = along_x(activations, 1), along_x(activations, -1)
    over_a = across_z(activations[:ROWS_A])
    over_left_a, over_right_a = along_x(over_a, 1), along_x(over_a, -1)
    over_b = across_z(activations[ROWS_A:])
    far0, far1 = along_x(left[:FAR], 1), along_x(right[FAR:], -1)
    over_b2 = across_z(jnp.concatenate([left[ROWS_A:], right[ROWS_A:]]))
    before, zero = early_call(common, 0, [activations, left, right, over_a, over_b])
    over_far0 = along_x(lax.dynamic_slice_in_dim(over_left_a, zero[0], FAR_A), 1)
    over_far1 = along_x(
        lax.dynamic_slice_in_dim(over_right_a, zero[0] + FAR_A, ROWS_A - FAR_A), -1
    )
    over_far_b = across_z(
        lax.dynamic_slice_in_dim(far1, zero[0] + ROWS_A - FAR, BLOCK - ROWS_A)
    )
    rows_b = BLOCK - ROWS_A
    late = [far0, far1, over_left_a, (over_b2, 0, rows_b), over_right_a, (over_b2, rows_b, rows_b)]
    late_rotated = late_call(common, 4, late)
    mine, theirs = renew_call(
        common, 7, before, late_rotated, late, [over_far0, over_far1, over_far_b]
    )

    theirs = to_other_core(theirs)
    summed = None
    for step_y, step_z in ((2, 1), (1, 1), (3, 1), (1, 0), (3, 0), (2, 0), (0, 1), (0, 0)):
        index = step_y * 2 + step_z
        pair = mine[index].astype(jnp.float32) + theirs[index].astype(jnp.float32)
        if index:
            pair = to_chip(pair.astype(jnp.bfloat16), step_y, step_z).astype(jnp.float32)
        summed = pair if summed is None else summed + pair
    summed = summed.reshape(outer_weight.shape)

    mean_weight = summed / lax.axis_size("rep")
    pseudo = outer_weight - mean_weight
    new_momentum = 0.9 * momentum + pseudo
    new_outer = outer_weight - 0.7 * (pseudo + 0.9 * new_momentum)
    new_average = 0.9 * average_weight + 0.1 * new_outer
    return (new_outer, new_momentum, new_average)


def solution(mesh):
    placed = (
        P(("rep", "grp"), None),
        P("rep"),
        P("rep", "grp"),
        P("rep", "grp", None, None),
        P(),
        P("grp", "rep", None),
        P("grp", "rep", None),
        P("grp", "rep", None),
    )
    return jax.shard_map(
        shards,
        mesh=mesh,
        in_specs=placed,
        out_specs=(P("grp", "rep", None), P("grp", "rep", None), P("grp", "rep", None)),
        check_vma=False,
    )
```

```python
import functools
import math

import jax
import jax.numpy as jnp
from jax import lax
from jax.experimental import pallas as pl
from jax.experimental.pallas import tpu as pltpu
from jax.sharding import PartitionSpec as P

ITERS = 5
COEF_A = 3.4445
COEF_B = -4.775
COEF_C = 2.0315

RING = 4
BLOCK = 128
ROWS_A = 80
FAR, FAR_A = 64, 48
TILE = 1280
EARLY_VMEM, LATE_VMEM, RENEW_VMEM, PICK_VMEM = 18, 12, 26, 8


def along_x(array, step):
    pairs = [(z * RING + x, z * RING + (x + step) % RING) for z in range(2) for x in range(RING)]
    return lax.ppermute(array, "grp", pairs)


def across_z(array):
    return lax.ppermute(array, "grp", [(g, (g + RING) % (2 * RING)) for g in range(2 * RING)])


def to_other_core(array):
    return lax.ppermute(array, "rep", [(r, r ^ 1) for r in range(16)])


def to_chip(array, step_y, step_z):
    pairs = []
    for y in range(4):
        for z in range(2):
            for core in range(2):
                source = (y * 2 + z) * 2 + core
                target = (((y + step_y) % 4) * 2 + (z + step_z) % 2) * 2 + core
                pairs.append((source, target))
    return lax.ppermute(array, "rep", pairs)


def contract(left, right, left_dim, right_dim):
    return lax.dot_general(
        left, right, (((left_dim,), (right_dim,)), ((), ())), preferred_element_type=jnp.float32
    )


def halves(value):
    high = value.astype(jnp.bfloat16)
    return high, (value - high.astype(jnp.float32)).astype(jnp.bfloat16)


def product(left, right):
    high, low = left
    right_high, right_low = right
    wide = contract(
        jnp.concatenate([high, low], 1), jnp.concatenate([right_high, right_high], 0), 1, 0
    )
    return wide + contract(high, right_low, 1, 0)


def orthogonal_factors(grams, width):
    size = grams[0].shape[0]
    eye = (
        lax.broadcasted_iota(jnp.int32, (size, size), 0)
        == lax.broadcasted_iota(jnp.int32, (size, size), 1)
    ).astype(jnp.float32)
    scales, current = [], []
    for gram in grams:
        square_sum = jnp.sum(gram * eye, keepdims=True)
        scale = 1.0 / (jnp.sqrt(square_sum) + 1e-07)
        scales.append(scale)
        current.append(gram * scale * scale)
    totals = None
    for number in range(ITERS):
        split = [halves(gram) for gram in current]
        squares = [product(gram, gram) for gram in split]
        steps = [
            COEF_A * eye + COEF_B * gram + COEF_C * square for gram, square in zip(current, squares)
        ]
        step_split = [halves(step) for step in steps]
        if totals is None:
            totals_next = steps
        else:
            total_split = [halves(total) for total in totals]
            totals_next = [product(s, t) for s, t in zip(step_split, total_split)]
        if number < ITERS - 1:
            half = [halves(product(s, g)) for s, g in zip(step_split, split)]
            current = [product(h, s) for h, s in zip(half, step_split)]
        totals = totals_next
    factor = 0.2 * math.sqrt(width)
    return [total * (scale * factor) for total, scale in zip(totals, scales)]


class Copies:
    def __init__(self, sems):
        self.sems, self.count = sems, 0

    def start(self, source, target):
        copy = pltpu.make_async_copy(source, target, self.sems.at[self.count])
        copy.start()
        self.count += 1
        return copy


def start_tokens(copies, pieces, spans, tokens, offset=0):
    started = []
    for piece, (begin, count) in zip(pieces, spans):
        target = tokens.at[pl.ds(offset, count)]
        started.append(copies.start(piece.at[pl.ds(begin, count)], target))
        offset += count
    return started


def start_upstream(copies, place_ref, first_block, upstream_ref, upstream):
    started = []
    for block in range(upstream.shape[0] // BLOCK):
        begin = pl.multiple_of(place_ref[first_block + block] * BLOCK, BLOCK)
        target = upstream.at[pl.ds(block * BLOCK, BLOCK)]
        started.append(copies.start(upstream_ref.at[pl.ds(begin, BLOCK)], target))
    return started


def wait_all(copies):
    for copy in copies:
        copy.wait()


def head_gradient(queries, scaled):
    inverse = lax.rsqrt(jnp.mean(queries * queries, axis=0, keepdims=True) + 1e-06)
    normed = queries * inverse
    projection = jnp.mean(normed * scaled, axis=0, keepdims=True)
    return (scaled - normed * projection) * inverse


def rotated_gradient(
    place_ref, first_block, gain_ref, ids_ref, tokens, weight, upstream, turned, rotated, base, ready
):
    rows = upstream.shape[0]
    size = gain_ref.shape[1]
    heads = weight.shape[0] // size
    gain = jnp.broadcast_to(gain_ref[...], (BLOCK, size)).T
    for block in range(rows // BLOCK):
        span = slice(block * BLOCK, (block + 1) * BLOCK)
        for head in range(heads):
            columns = slice(head * size, (head + 1) * size)
            turned[columns, span] = gain * upstream[span, columns].astype(jnp.float32).T
    live = []
    for block in range(rows // BLOCK):
        ids = ids_ref[pl.ds(place_ref[first_block + block], 1), :]
        live.append((ids != 0).astype(jnp.float32))
    live = jnp.concatenate(live, 1)
    wait_all(ready)
    for begin in range(0, rows, 2 * BLOCK):
        count = min(2 * BLOCK, rows - begin)
        span = pl.ds(base + begin, count)
        there = slice(begin, begin + count)
        queries = contract(weight[...], tokens[span, :], 1, 1)
        for head in range(heads):
            columns = slice(head * size, (head + 1) * size)
            grad = head_gradient(queries[columns], turned[columns, there])
            rotated[columns, span] = (grad * live[:, there]).astype(jnp.bfloat16)


def early_kernel(first_block, spans, *refs):
    count = len(spans)
    place_ref, gain_ref, ids_ref, upstream_ref, weight = refs[:5]
    pieces, refs = refs[5 : 5 + count], refs[5 + count :]
    _, out_ref, _, tokens, upstream, turned, rotated, sems = refs
    copies = Copies(sems)
    needed = start_upstream(copies, place_ref, first_block, upstream_ref, upstream)
    ready = start_tokens(copies, pieces, spans, tokens)
    wait_all(needed)
    rotated_gradient(
        place_ref, first_block, gain_ref, ids_ref, tokens, weight, upstream, turned, rotated, 0, ready
    )

    @pl.loop(0, out_ref.shape[1] // TILE)
    def _(tile):
        columns = pl.ds(pl.multiple_of(tile * TILE, TILE), TILE)
        out_ref[:, columns] = contract(rotated[...], tokens[:, columns], 1, 0)


def late_kernel(first_block, spans, *refs):
    count = len(spans)
    place_ref, gain_ref, ids_ref, upstream_ref, weight = refs[:5]
    pieces, refs = refs[5 : 5 + count], refs[5 + count :]
    out_ref, tokens, upstream, turned, sems = refs
    copies = Copies(sems)
    needed = start_upstream(copies, place_ref, first_block, upstream_ref, upstream)
    ready = start_tokens(copies, pieces, spans, tokens)
    wait_all(needed)
    rotated_gradient(
        place_ref, first_block, gain_ref, ids_ref, tokens, weight, upstream, turned, out_ref, 0, ready
    )


def renew_kernel(first_block, late_spans, spans, *refs):
    late_count, count = len(late_spans), len(spans)
    place_ref, gain_ref, ids_ref, upstream_ref, weight, before_ref, late_ref = refs[:7]
    late, refs = refs[7 : 7 + late_count], refs[7 + late_count :]
    pieces, (mine_ref, theirs_ref) = refs[:count], refs[count : count + 2]
    tokens, upstream, turned, rotated, split, factors, sems = refs[count + 2 :]
    all_rows, width = weight.shape
    size = gain_ref.shape[1]
    heads = all_rows // size
    tiles = width // TILE
    rows = upstream.shape[0]
    late_rows = tokens.shape[0] - rows
    copies = Copies(sems)
    needed = start_upstream(copies, place_ref, first_block, upstream_ref, upstream)
    ready = start_tokens(copies, pieces, spans, tokens, late_rows)
    others = start_tokens(copies, late, late_spans, tokens)
    rotated[:, :late_rows] = late_ref[...]
    wait_all(needed)
    rotated_gradient(
        place_ref, first_block, gain_ref, ids_ref, tokens, weight, upstream, turned, rotated,
        late_rows, ready,
    )
    wait_all(others)

    @pl.loop(0, tiles)
    def _(tile):
        columns = pl.ds(pl.multiple_of(tile * TILE, TILE), TILE)
        part = contract(rotated[...], tokens[:, columns], 1, 0) + before_ref[:, columns]
        high, low = halves(part)
        for head in range(heads):
            span = slice(head * size, (head + 1) * size)
            split[head, :size, columns] = high[span]
            split[head, size:, columns] = low[span]

    grams = []
    for head in range(heads):
        both = split[head]
        whole = contract(both, both, 1, 1)
        grams.append(
            whole[:size, :size] + whole[:size, size:] + whole[size:, :size] + whole[size:, size:]
        )
    for head, factor in enumerate(orthogonal_factors(grams, width)):
        high, low = halves(factor)
        factors[head, :size, :size] = high
        factors[head, :size, size:] = high
        factors[head, size:, :size] = low
        factors[head, size:, size:] = jnp.zeros_like(low)

    core_is_zero = place_ref[10] == 0
    indices = []
    for chip in range(8):
        step_y = lax.rem(chip // 2 - place_ref[8] + 4, 4)
        step_z = lax.rem(chip % 2 - place_ref[9] + 2, 2)
        indices.append(step_y * 2 + step_z)

    @pl.loop(0, tiles)
    def _(tile):
        columns = pl.ds(pl.multiple_of(tile * TILE, TILE), TILE)
        for pair in range(heads // 2):
            renewed = []
            for head in (2 * pair, 2 * pair + 1):
                both = contract(factors[head], split[head, :, columns], 1, 0)
                change = both[:size] + both[size:]
                old = weight[head * size : (head + 1) * size, columns].astype(jnp.float32)
                renewed.append(old - change)
            span = pl.ds(pair * 16, 16)
            for chip, index in enumerate(indices):
                parts = []
                for core in range(2):
                    begin = (chip * 2 + core) * 8
                    parts.append(
                        jnp.concatenate([value[begin : begin + 8] for value in renewed], 0)
                    )
                mine = jnp.where(core_is_zero, parts[0], parts[1])
                theirs = jnp.where(core_is_zero, parts[1], parts[0])
                mine_ref[index, span, columns] = mine.astype(jnp.bfloat16)
                theirs_ref[index, span, columns] = theirs.astype(jnp.bfloat16)


OUTSIDE = pl.BlockSpec(memory_space=pltpu.HBM)
INSIDE = pl.BlockSpec(memory_space=pltpu.VMEM)
SCALARS = pl.BlockSpec(memory_space=pltpu.SMEM)


def outside(array):
    return pltpu.with_memory_space_constraint(array, pltpu.HBM)


def call(kernel, out_shape, in_specs, out_specs, scratch, flops, moved, vmem, operands, aliases=None):
    return pl.pallas_call(
        kernel,
        out_shape=out_shape,
        in_specs=in_specs,
        out_specs=out_specs,
        scratch_shapes=scratch,
        input_output_aliases=aliases or {},
        compiler_params=pltpu.CompilerParams(vmem_limit_bytes=vmem * 1024 * 1024),
        cost_estimate=pl.CostEstimate(flops=flops, bytes_accessed=moved, transcendentals=0),
    )(*operands)


def scratch_of(common, rows):
    all_rows, width = common[-1].shape
    return [
        pltpu.VMEM((rows, all_rows), jnp.bfloat16),
        pltpu.VMEM((all_rows, rows), jnp.float32),
    ]


def arrays_of(pieces):
    return [outside(piece[0] if isinstance(piece, tuple) else piece) for piece in pieces]


def spans_of(pieces):
    return [piece[1:] if isinstance(piece, tuple) else (0, piece.shape[0]) for piece in pieces]


def rows_of(pieces):
    return sum(count for _, count in spans_of(pieces))


COMMON_SPECS = [SCALARS, INSIDE, INSIDE, OUTSIDE, INSIDE]


def pick_kernel(picks, count, *refs):
    sources, targets, sems = refs[:count], refs[-1 - len(picks) : -1], refs[-1]
    copies = Copies(sems)
    started = []
    for target, parts in zip(targets, picks):
        offset = 0
        for number, begin, rows in parts:
            source = sources[number].at[pl.ds(begin, rows)]
            started.append(copies.start(source, target.at[pl.ds(offset, rows)]))
            offset += rows
    wait_all(started)


def pick_call(arrays, picks):
    shapes = []
    for parts in picks:
        rows = sum(part[2] for part in parts)
        shapes.append(jax.ShapeDtypeStruct((rows, arrays[0].shape[1]), arrays[0].dtype))
    moved = 4 * sum(shape.size for shape in shapes)
    scratch = [pltpu.SemaphoreType.DMA((sum(len(parts) for parts in picks),))]
    return call(
        functools.partial(pick_kernel, picks, len(arrays)),
        tuple(shapes),
        [OUTSIDE] * len(arrays),
        (INSIDE,) * len(shapes),
        scratch,
        0,
        moved,
        PICK_VMEM,
        list(map(outside, arrays)),
    )


def early_call(common, first_block, pieces, passed):
    all_rows, width = common[-1].shape
    rows = rows_of(pieces)
    return call(
        functools.partial(early_kernel, first_block, spans_of(pieces)),
        (
            jax.ShapeDtypeStruct((all_rows, width), jnp.float32),
            jax.ShapeDtypeStruct(passed.shape, passed.dtype),
        ),
        COMMON_SPECS + [OUTSIDE] * (len(pieces) + 1),
        (INSIDE, OUTSIDE),
        [pltpu.VMEM((rows, width), jnp.bfloat16)]
        + scratch_of(common, rows)
        + [
            pltpu.VMEM((all_rows, rows), jnp.bfloat16),
            pltpu.SemaphoreType.DMA((len(pieces) + rows // BLOCK,)),
        ],
        4 * rows * all_rows * width,
        (6 * all_rows + 2 * rows) * width,
        EARLY_VMEM,
        [*common, *arrays_of(pieces), passed],
        {len(common) + len(pieces): 1},
    )


def late_call(common, first_block, pieces):
    all_rows, width = common[-1].shape
    rows = rows_of(pieces)
    return call(
        functools.partial(late_kernel, first_block, spans_of(pieces)),
        jax.ShapeDtypeStruct((all_rows, rows), jnp.bfloat16),
        COMMON_SPECS + [OUTSIDE] * len(pieces),
        INSIDE,
        [pltpu.VMEM((rows, width), jnp.bfloat16)]
        + scratch_of(common, rows)
        + [pltpu.SemaphoreType.DMA((len(pieces) + rows // BLOCK,))],
        2 * rows * all_rows * width,
        2 * (rows + all_rows) * width,
        LATE_VMEM,
        [*common, *arrays_of(pieces)],
    )


def renew_call(common, first_block, before, late_rotated, late, pieces):
    all_rows, width = common[-1].shape
    size = common[1].shape[1]
    heads = all_rows // size
    rows = rows_of(pieces)
    total = rows + rows_of(late)
    shape = jax.ShapeDtypeStruct((8, all_rows // 16, width), jnp.bfloat16)
    return call(
        functools.partial(renew_kernel, first_block, spans_of(late), spans_of(pieces)),
        (shape, shape),
        COMMON_SPECS + [INSIDE, INSIDE] + [OUTSIDE] * (len(late) + len(pieces)),
        (INSIDE, INSIDE),
        [pltpu.VMEM((total, width), jnp.bfloat16)]
        + scratch_of(common, rows)
        + [
            pltpu.VMEM((all_rows, total), jnp.bfloat16),
            pltpu.VMEM((heads, 2 * size, width), jnp.bfloat16),
            pltpu.VMEM((heads, 2 * size, 2 * size), jnp.bfloat16),
            pltpu.SemaphoreType.DMA((len(late) + len(pieces) + rows // BLOCK,)),
        ],
        (4 * rows + 16 * size) * all_rows * width,
        8 * all_rows * width,
        RENEW_VMEM,
        [*common, before, late_rotated, *arrays_of(late), *arrays_of(pieces)],
    )


def shards(
    activations,
    token_ids,
    cotangent,
    inner_weight,
    query_gain,
    outer_weight,
    momentum,
    average_weight,
):
    weights = inner_weight[0]
    head_count, head_size, model_width = weights.shape
    flat_weight = weights.reshape(head_count * head_size, model_width)

    place = lax.axis_index("grp")
    spot = lax.axis_index("rep")
    numbers = []
    for step_z, step_x in ((0, 0), (0, -1), (0, 1), (1, 0), (0, 2), (1, -1), (1, 1), (1, 2)):
        numbers.append(((place // RING + step_z) % 2) * RING + (place + step_x) % RING)
    numbers += [spot // 4, (spot // 2) % 2, spot % 2]
    common = (
        jnp.stack(numbers).astype(jnp.int32),
        query_gain[None, :],
        token_ids.reshape(2 * RING, BLOCK),
        outside(cotangent),
        flat_weight,
    )

    rows_b = BLOCK - ROWS_A
    left, right = along_x(activations, 1), along_x(activations, -1)
    own_a, own_b = pick_call([activations], [[(0, 0, ROWS_A)], [(0, ROWS_A, rows_b)]])
    over_a = across_z(own_a)
    over_left_a, over_right_a = along_x(over_a, 1), along_x(over_a, -1)
    over_b = across_z(own_b)
    left_far, right_far, right_b, sides_b = pick_call(
        [left, right],
        [
            [(0, 0, FAR)],
            [(1, FAR, ROWS_A - FAR)],
            [(1, ROWS_A, rows_b)],
            [(0, ROWS_A, rows_b), (1, ROWS_A, rows_b)],
        ],
    )
    far_b = along_x(right_b, -1)
    far0 = along_x(left_far, 1)
    over_b2 = across_z(sides_b)
    before, right_far = early_call(common, 0, [activations, left, right, over_a, over_b], right_far)
    over_left_far, over_right_far, right_far = pick_call(
        [over_left_a, over_right_a, right_far],
        [[(0, 0, FAR_A)], [(1, FAR_A, ROWS_A - FAR_A)], [(2, 0, ROWS_A - FAR)]],
    )
    over_far0, over_far1 = along_x(over_left_far, 1), along_x(over_right_far, -1)
    far1 = along_x(right_far, -1)
    over_far_b = across_z(far_b)
    late = [
        far0, far1, far_b, over_left_a, (over_b2, 0, rows_b), over_right_a, (over_b2, rows_b, rows_b)
    ]
    late_rotated = late_call(common, 4, late)
    mine, theirs = renew_call(
        common, 7, before, late_rotated, late, [over_far0, over_far1, over_far_b]
    )

    theirs = to_other_core(theirs)
    summed = None
    for step_y, step_z in ((0, 1), (2, 1), (2, 0), (3, 1), (1, 1), (3, 0), (1, 0), (0, 0)):
        index = step_y * 2 + step_z
        pair = mine[index].astype(jnp.float32) + theirs[index].astype(jnp.float32)
        if index:
            pair = to_chip(pair.astype(jnp.bfloat16), step_y, step_z).astype(jnp.float32)
        summed = pair if summed is None else summed + pair
    summed = summed.reshape(outer_weight.shape)

    mean_weight = summed / lax.axis_size("rep")
    pseudo = outer_weight - mean_weight
    new_momentum = 0.9 * momentum + pseudo
    new_outer = outer_weight - 0.7 * (pseudo + 0.9 * new_momentum)
    new_average = 0.9 * average_weight + 0.1 * new_outer
    return (new_outer, new_momentum, new_average)


def solution(mesh):
    placed = (
        P(("rep", "grp"), None),
        P("rep"),
        P("rep", "grp"),
        P("rep", "grp", None, None),
        P(),
        P("grp", "rep", None),
        P("grp", "rep", None),
        P("grp", "rep", None),
    )
    return jax.shard_map(
        shards,
        mesh=mesh,
        in_specs=placed,
        out_specs=(P("grp", "rep", None), P("grp", "rep", None), P("grp", "rep", None)),
        check_vma=False,
    )
```

```python
import functools
import math

import jax
import jax.numpy as jnp
from jax import lax
from jax.experimental import pallas as pl
from jax.experimental.pallas import tpu as pltpu
from jax.sharding import PartitionSpec as P

ITERS = 5
COEF_A = 3.4445
COEF_B = -4.775
COEF_C = 2.0315

RING = 4
BLOCK = 128
ROWS_A = 80
FAR, FAR_A = 64, 48
TILE = 2560
EARLY_VMEM, LATE_VMEM, RENEW_VMEM, PICK_VMEM = 18, 12, 26, 8


def along_x(array, step):
    pairs = [(z * RING + x, z * RING + (x + step) % RING) for z in range(2) for x in range(RING)]
    return lax.ppermute(array, "grp", pairs)


def across_z(array):
    return lax.ppermute(array, "grp", [(g, (g + RING) % (2 * RING)) for g in range(2 * RING)])


def to_other_core(array):
    return lax.ppermute(array, "rep", [(r, r ^ 1) for r in range(16)])


def to_chip(array, step_y, step_z):
    pairs = []
    for y in range(4):
        for z in range(2):
            for core in range(2):
                source = (y * 2 + z) * 2 + core
                target = (((y + step_y) % 4) * 2 + (z + step_z) % 2) * 2 + core
                pairs.append((source, target))
    return lax.ppermute(array, "rep", pairs)


def contract(left, right, left_dim, right_dim):
    return lax.dot_general(
        left, right, (((left_dim,), (right_dim,)), ((), ())), preferred_element_type=jnp.float32
    )


def halves(value):
    high = value.astype(jnp.bfloat16)
    return high, (value - high.astype(jnp.float32)).astype(jnp.bfloat16)


def product(left, right):
    high, low = left
    right_high, right_low = right
    wide = contract(
        jnp.concatenate([high, low], 1), jnp.concatenate([right_high, right_high], 0), 1, 0
    )
    return wide + contract(high, right_low, 1, 0)


def orthogonal_factors(grams, width):
    size = grams[0].shape[0]
    eye = (
        lax.broadcasted_iota(jnp.int32, (size, size), 0)
        == lax.broadcasted_iota(jnp.int32, (size, size), 1)
    ).astype(jnp.float32)
    scales, current = [], []
    for gram in grams:
        square_sum = jnp.sum(gram * eye, keepdims=True)
        scale = 1.0 / (jnp.sqrt(square_sum) + 1e-07)
        scales.append(scale)
        current.append(gram * scale * scale)
    totals = None
    for number in range(ITERS):
        split = [halves(gram) for gram in current]
        squares = [product(gram, gram) for gram in split]
        steps = [
            COEF_A * eye + COEF_B * gram + COEF_C * square for gram, square in zip(current, squares)
        ]
        step_split = [halves(step) for step in steps]
        if totals is None:
            totals_next = steps
        else:
            total_split = [halves(total) for total in totals]
            totals_next = [product(s, t) for s, t in zip(step_split, total_split)]
        if number < ITERS - 1:
            half = [halves(product(s, g)) for s, g in zip(step_split, split)]
            current = [product(h, s) for h, s in zip(half, step_split)]
        totals = totals_next
    factor = 0.2 * math.sqrt(width)
    return [total * (scale * factor) for total, scale in zip(totals, scales)]


class Copies:
    def __init__(self, sems):
        self.sems, self.count = sems, 0

    def start(self, source, target):
        copy = pltpu.make_async_copy(source, target, self.sems.at[self.count])
        copy.start()
        self.count += 1
        return copy


def start_tokens(copies, pieces, spans, tokens, offset=0):
    started = []
    for piece, (begin, count) in zip(pieces, spans):
        target = tokens.at[pl.ds(offset, count)]
        started.append(copies.start(piece.at[pl.ds(begin, count)], target))
        offset += count
    return started


def start_upstream(copies, place_ref, first_block, upstream_ref, upstream):
    started = []
    for block in range(upstream.shape[0] // BLOCK):
        begin = pl.multiple_of(place_ref[first_block + block] * BLOCK, BLOCK)
        target = upstream.at[pl.ds(block * BLOCK, BLOCK)]
        started.append(copies.start(upstream_ref.at[pl.ds(begin, BLOCK)], target))
    return started


def wait_all(copies):
    for copy in copies:
        copy.wait()


def head_gradient(queries, scaled):
    inverse = lax.rsqrt(jnp.mean(queries * queries, axis=0, keepdims=True) + 1e-06)
    normed = queries * inverse
    projection = jnp.mean(normed * scaled, axis=0, keepdims=True)
    return (scaled - normed * projection) * inverse


def rotated_gradient(
    place_ref, first_block, gain_ref, ids_ref, tokens, weight, upstream, turned, rotated, base, ready
):
    rows = upstream.shape[0]
    size = gain_ref.shape[1]
    heads = weight.shape[0] // size
    gain = jnp.broadcast_to(gain_ref[...], (BLOCK, size)).T
    for block in range(rows // BLOCK):
        span = slice(block * BLOCK, (block + 1) * BLOCK)
        for head in range(heads):
            columns = slice(head * size, (head + 1) * size)
            turned[columns, span] = gain * upstream[span, columns].astype(jnp.float32).T
    live = []
    for block in range(rows // BLOCK):
        ids = ids_ref[pl.ds(place_ref[first_block + block], 1), :]
        live.append((ids != 0).astype(jnp.float32))
    live = jnp.concatenate(live, 1)
    wait_all(ready)
    for begin in range(0, rows, 2 * BLOCK):
        count = min(2 * BLOCK, rows - begin)
        span = pl.ds(base + begin, count)
        there = slice(begin, begin + count)
        queries = contract(weight[...], tokens[span, :], 1, 1)
        for head in range(heads):
            columns = slice(head * size, (head + 1) * size)
            grad = head_gradient(queries[columns], turned[columns, there])
            rotated[columns, span] = (grad * live[:, there]).astype(jnp.bfloat16)


def early_kernel(first_block, spans, *refs):
    count = len(spans)
    place_ref, gain_ref, ids_ref, upstream_ref, weight = refs[:5]
    pieces, refs = refs[5 : 5 + count], refs[5 + count :]
    _, out_ref, _, tokens, upstream, turned, rotated, sems = refs
    copies = Copies(sems)
    needed = start_upstream(copies, place_ref, first_block, upstream_ref, upstream)
    ready = start_tokens(copies, pieces, spans, tokens)
    wait_all(needed)
    rotated_gradient(
        place_ref, first_block, gain_ref, ids_ref, tokens, weight, upstream, turned, rotated, 0, ready
    )

    @pl.loop(0, out_ref.shape[1] // TILE)
    def _(tile):
        columns = pl.ds(pl.multiple_of(tile * TILE, TILE), TILE)
        out_ref[:, columns] = contract(rotated[...], tokens[:, columns], 1, 0)


def late_kernel(first_block, spans, *refs):
    count = len(spans)
    place_ref, gain_ref, ids_ref, upstream_ref, weight = refs[:5]
    pieces, refs = refs[5 : 5 + count], refs[5 + count :]
    out_ref, tokens, upstream, turned, sems = refs
    copies = Copies(sems)
    needed = start_upstream(copies, place_ref, first_block, upstream_ref, upstream)
    ready = start_tokens(copies, pieces, spans, tokens)
    wait_all(needed)
    rotated_gradient(
        place_ref, first_block, gain_ref, ids_ref, tokens, weight, upstream, turned, out_ref, 0, ready
    )


def renew_kernel(first_block, late_spans, spans, *refs):
    late_count, count = len(late_spans), len(spans)
    place_ref, gain_ref, ids_ref, upstream_ref, weight, before_ref, late_ref = refs[:7]
    late, refs = refs[7 : 7 + late_count], refs[7 + late_count :]
    pieces, (mine_ref, theirs_ref) = refs[:count], refs[count : count + 2]
    tokens, upstream, turned, rotated, split, factors, sems = refs[count + 2 :]
    all_rows, width = weight.shape
    size = gain_ref.shape[1]
    heads = all_rows // size
    tiles = width // TILE
    rows = upstream.shape[0]
    late_rows = tokens.shape[0] - rows
    copies = Copies(sems)
    needed = start_upstream(copies, place_ref, first_block, upstream_ref, upstream)
    ready = start_tokens(copies, pieces, spans, tokens, late_rows)
    others = start_tokens(copies, late, late_spans, tokens)
    rotated[:, :late_rows] = late_ref[...]
    wait_all(needed)
    rotated_gradient(
        place_ref, first_block, gain_ref, ids_ref, tokens, weight, upstream, turned, rotated,
        late_rows, ready,
    )
    wait_all(others)

    @pl.loop(0, tiles)
    def _(tile):
        columns = pl.ds(pl.multiple_of(tile * TILE, TILE), TILE)
        part = contract(rotated[...], tokens[:, columns], 1, 0) + before_ref[:, columns]
        high, low = halves(part)
        for head in range(heads):
            span = slice(head * size, (head + 1) * size)
            split[head, :size, columns] = high[span]
            split[head, size:, columns] = low[span]

    grams = []
    for head in range(heads):
        both = split[head]
        whole = contract(both, both, 1, 1)
        grams.append(
            whole[:size, :size] + whole[:size, size:] + whole[size:, :size] + whole[size:, size:]
        )
    for head, factor in enumerate(orthogonal_factors(grams, width)):
        high, low = halves(factor)
        factors[head, :size, :size] = high
        factors[head, :size, size:] = high
        factors[head, size:, :size] = low
        factors[head, size:, size:] = jnp.zeros_like(low)

    core_is_zero = place_ref[10] == 0
    indices = []
    for chip in range(8):
        step_y = lax.rem(chip // 2 - place_ref[8] + 4, 4)
        step_z = lax.rem(chip % 2 - place_ref[9] + 2, 2)
        indices.append(step_y * 2 + step_z)

    @pl.loop(0, tiles)
    def _(tile):
        columns = pl.ds(pl.multiple_of(tile * TILE, TILE), TILE)
        for pair in range(heads // 2):
            renewed = []
            for head in (2 * pair, 2 * pair + 1):
                both = contract(factors[head], split[head, :, columns], 1, 0)
                change = both[:size] + both[size:]
                old = weight[head * size : (head + 1) * size, columns].astype(jnp.float32)
                renewed.append(old - change)
            span = pl.ds(pair * 16, 16)
            for chip, index in enumerate(indices):
                parts = []
                for core in range(2):
                    begin = (chip * 2 + core) * 8
                    parts.append(
                        jnp.concatenate([value[begin : begin + 8] for value in renewed], 0)
                    )
                mine = jnp.where(core_is_zero, parts[0], parts[1])
                theirs = jnp.where(core_is_zero, parts[1], parts[0])
                mine_ref[index, span, columns] = mine.astype(jnp.bfloat16)
                theirs_ref[index, span, columns] = theirs.astype(jnp.bfloat16)


OUTSIDE = pl.BlockSpec(memory_space=pltpu.HBM)
INSIDE = pl.BlockSpec(memory_space=pltpu.VMEM)
SCALARS = pl.BlockSpec(memory_space=pltpu.SMEM)


def outside(array):
    return pltpu.with_memory_space_constraint(array, pltpu.HBM)


def call(kernel, out_shape, in_specs, out_specs, scratch, flops, moved, vmem, operands, aliases=None):
    return pl.pallas_call(
        kernel,
        out_shape=out_shape,
        in_specs=in_specs,
        out_specs=out_specs,
        scratch_shapes=scratch,
        input_output_aliases=aliases or {},
        compiler_params=pltpu.CompilerParams(vmem_limit_bytes=vmem * 1024 * 1024),
        cost_estimate=pl.CostEstimate(flops=flops, bytes_accessed=moved, transcendentals=0),
    )(*operands)


def scratch_of(common, rows):
    all_rows, width = common[-1].shape
    return [
        pltpu.VMEM((rows, all_rows), jnp.bfloat16),
        pltpu.VMEM((all_rows, rows), jnp.float32),
    ]


def arrays_of(pieces):
    return [outside(piece[0] if isinstance(piece, tuple) else piece) for piece in pieces]


def spans_of(pieces):
    return [piece[1:] if isinstance(piece, tuple) else (0, piece.shape[0]) for piece in pieces]


def rows_of(pieces):
    return sum(count for _, count in spans_of(pieces))


COMMON_SPECS = [SCALARS, INSIDE, INSIDE, OUTSIDE, INSIDE]


def pick_kernel(picks, count, *refs):
    sources, targets, sems = refs[:count], refs[-1 - len(picks) : -1], refs[-1]
    copies = Copies(sems)
    started = []
    for target, parts in zip(targets, picks):
        offset = 0
        for number, begin, rows in parts:
            source = sources[number].at[pl.ds(begin, rows)]
            started.append(copies.start(source, target.at[pl.ds(offset, rows)]))
            offset += rows
    wait_all(started)


def pick_call(arrays, picks):
    shapes = []
    for parts in picks:
        rows = sum(part[2] for part in parts)
        shapes.append(jax.ShapeDtypeStruct((rows, arrays[0].shape[1]), arrays[0].dtype))
    moved = 4 * sum(shape.size for shape in shapes)
    scratch = [pltpu.SemaphoreType.DMA((sum(len(parts) for parts in picks),))]
    return call(
        functools.partial(pick_kernel, picks, len(arrays)),
        tuple(shapes),
        [OUTSIDE] * len(arrays),
        (INSIDE,) * len(shapes),
        scratch,
        0,
        moved,
        PICK_VMEM,
        list(map(outside, arrays)),
    )


def early_call(common, first_block, pieces, passed):
    all_rows, width = common[-1].shape
    rows = rows_of(pieces)
    return call(
        functools.partial(early_kernel, first_block, spans_of(pieces)),
        (
            jax.ShapeDtypeStruct((all_rows, width), jnp.float32),
            jax.ShapeDtypeStruct(passed.shape, passed.dtype),
        ),
        COMMON_SPECS + [OUTSIDE] * (len(pieces) + 1),
        (INSIDE, OUTSIDE),
        [pltpu.VMEM((rows, width), jnp.bfloat16)]
        + scratch_of(common, rows)
        + [
            pltpu.VMEM((all_rows, rows), jnp.bfloat16),
            pltpu.SemaphoreType.DMA((len(pieces) + rows // BLOCK,)),
        ],
        4 * rows * all_rows * width,
        (6 * all_rows + 2 * rows) * width,
        EARLY_VMEM,
        [*common, *arrays_of(pieces), passed],
        {len(common) + len(pieces): 1},
    )


def late_call(common, first_block, pieces):
    all_rows, width = common[-1].shape
    rows = rows_of(pieces)
    return call(
        functools.partial(late_kernel, first_block, spans_of(pieces)),
        jax.ShapeDtypeStruct((all_rows, rows), jnp.bfloat16),
        COMMON_SPECS + [OUTSIDE] * len(pieces),
        INSIDE,
        [pltpu.VMEM((rows, width), jnp.bfloat16)]
        + scratch_of(common, rows)
        + [pltpu.SemaphoreType.DMA((len(pieces) + rows // BLOCK,))],
        2 * rows * all_rows * width,
        2 * (rows + all_rows) * width,
        LATE_VMEM,
        [*common, *arrays_of(pieces)],
    )


def renew_call(common, first_block, before, late_rotated, late, pieces):
    all_rows, width = common[-1].shape
    size = common[1].shape[1]
    heads = all_rows // size
    rows = rows_of(pieces)
    total = rows + rows_of(late)
    shape = jax.ShapeDtypeStruct((8, all_rows // 16, width), jnp.bfloat16)
    return call(
        functools.partial(renew_kernel, first_block, spans_of(late), spans_of(pieces)),
        (shape, shape),
        COMMON_SPECS + [INSIDE, INSIDE] + [OUTSIDE] * (len(late) + len(pieces)),
        (INSIDE, INSIDE),
        [pltpu.VMEM((total, width), jnp.bfloat16)]
        + scratch_of(common, rows)
        + [
            pltpu.VMEM((all_rows, total), jnp.bfloat16),
            pltpu.VMEM((heads, 2 * size, width), jnp.bfloat16),
            pltpu.VMEM((heads, 2 * size, 2 * size), jnp.bfloat16),
            pltpu.SemaphoreType.DMA((len(late) + len(pieces) + rows // BLOCK,)),
        ],
        (4 * rows + 16 * size) * all_rows * width,
        8 * all_rows * width,
        RENEW_VMEM,
        [*common, before, late_rotated, *arrays_of(late), *arrays_of(pieces)],
    )


def shards(
    activations,
    token_ids,
    cotangent,
    inner_weight,
    query_gain,
    outer_weight,
    momentum,
    average_weight,
):
    weights = inner_weight[0]
    head_count, head_size, model_width = weights.shape
    flat_weight = weights.reshape(head_count * head_size, model_width)

    place = lax.axis_index("grp")
    spot = lax.axis_index("rep")
    numbers = []
    for step_z, step_x in ((0, 0), (0, -1), (0, 1), (1, 0), (0, 2), (1, -1), (1, 1), (1, 2)):
        numbers.append(((place // RING + step_z) % 2) * RING + (place + step_x) % RING)
    numbers += [spot // 4, (spot // 2) % 2, spot % 2]
    common = (
        jnp.stack(numbers).astype(jnp.int32),
        query_gain[None, :],
        token_ids.reshape(2 * RING, BLOCK),
        outside(cotangent),
        flat_weight,
    )

    rows_b = BLOCK - ROWS_A
    left, right = along_x(activations, 1), along_x(activations, -1)
    own_a, own_b = pick_call([activations], [[(0, 0, ROWS_A)], [(0, ROWS_A, rows_b)]])
    over_a = across_z(own_a)
    over_left_a, over_right_a = along_x(over_a, 1), along_x(over_a, -1)
    over_b = across_z(own_b)
    left_far, right_far, right_b, sides_b = pick_call(
        [left, right],
        [
            [(0, 0, FAR)],
            [(1, FAR, ROWS_A - FAR)],
            [(1, ROWS_A, rows_b)],
            [(0, ROWS_A, rows_b), (1, ROWS_A, rows_b)],
        ],
    )
    far_b = along_x(right_b, -1)
    far0 = along_x(left_far, 1)
    over_b2 = across_z(sides_b)
    before, right_far = early_call(common, 0, [activations, left, right, over_a, over_b], right_far)
    over_left_far, over_right_far, right_far = pick_call(
        [over_left_a, over_right_a, right_far],
        [[(0, 0, FAR_A)], [(1, FAR_A, ROWS_A - FAR_A)], [(2, 0, ROWS_A - FAR)]],
    )
    over_far0, over_far1 = along_x(over_left_far, 1), along_x(over_right_far, -1)
    far1 = along_x(right_far, -1)
    over_far_b = across_z(far_b)
    late = [
        far0, far1, far_b, over_left_a, (over_b2, 0, rows_b), over_right_a, (over_b2, rows_b, rows_b)
    ]
    late_rotated = late_call(common, 4, late)
    mine, theirs = renew_call(
        common, 7, before, late_rotated, late, [over_far0, over_far1, over_far_b]
    )

    theirs = to_other_core(theirs)
    summed = None
    for step_y, step_z in ((2, 1), (3, 1), (1, 0), (3, 0), (0, 1), (1, 1), (2, 0), (0, 0)):
        index = step_y * 2 + step_z
        pair = mine[index].astype(jnp.float32) + theirs[index].astype(jnp.float32)
        if index:
            pair = to_chip(pair.astype(jnp.bfloat16), step_y, step_z).astype(jnp.float32)
        summed = pair if summed is None else summed + pair
    summed = summed.reshape(outer_weight.shape)

    mean_weight = summed / lax.axis_size("rep")
    pseudo = outer_weight - mean_weight
    new_momentum = 0.9 * momentum + pseudo
    new_outer = outer_weight - 0.7 * (pseudo + 0.9 * new_momentum)
    new_average = 0.9 * average_weight + 0.1 * new_outer
    return (new_outer, new_momentum, new_average)


def solution(mesh):
    placed = (
        P(("rep", "grp"), None),
        P("rep"),
        P("rep", "grp"),
        P("rep", "grp", None, None),
        P(),
        P("grp", "rep", None),
        P("grp", "rep", None),
        P("grp", "rep", None),
    )
    return jax.shard_map(
        shards,
        mesh=mesh,
        in_specs=placed,
        out_specs=(P("grp", "rep", None), P("grp", "rep", None), P("grp", "rep", None)),
        check_vma=False,
    )
```

```python
import functools
import math

import jax
import jax.numpy as jnp
from jax import lax
from jax.experimental import pallas as pl
from jax.experimental.pallas import tpu as pltpu
from jax.sharding import PartitionSpec as P

ITERS = 5
COEF_A = 3.4445
COEF_B = -4.775
COEF_C = 2.0315

RING = 4
BLOCK = 128
ROWS_A = 80
FAR, FAR_A = 64, 48
TILE = 2560
EARLY_VMEM, LATE_VMEM, RENEW_VMEM, PICK_VMEM = 18, 12, 26, 8


def along_x(array, step):
    pairs = [(z * RING + x, z * RING + (x + step) % RING) for z in range(2) for x in range(RING)]
    return lax.ppermute(array, "grp", pairs)


def across_z(array):
    return lax.ppermute(array, "grp", [(g, (g + RING) % (2 * RING)) for g in range(2 * RING)])


def to_other_core(array):
    return lax.ppermute(array, "rep", [(r, r ^ 1) for r in range(16)])


def to_chip(array, step_y, step_z):
    pairs = []
    for y in range(4):
        for z in range(2):
            for core in range(2):
                source = (y * 2 + z) * 2 + core
                target = (((y + step_y) % 4) * 2 + (z + step_z) % 2) * 2 + core
                pairs.append((source, target))
    return lax.ppermute(array, "rep", pairs)


def contract(left, right, left_dim, right_dim):
    return lax.dot_general(
        left, right, (((left_dim,), (right_dim,)), ((), ())), preferred_element_type=jnp.float32
    )


def halves(value):
    high = value.astype(jnp.bfloat16)
    return high, (value - high.astype(jnp.float32)).astype(jnp.bfloat16)


def product(left, right):
    high, low = left
    right_high, right_low = right
    wide = contract(
        jnp.concatenate([high, low], 1), jnp.concatenate([right_high, right_high], 0), 1, 0
    )
    return wide + contract(high, right_low, 1, 0)


def orthogonal_factors(grams, width):
    size = grams[0].shape[0]
    eye = (
        lax.broadcasted_iota(jnp.int32, (size, size), 0)
        == lax.broadcasted_iota(jnp.int32, (size, size), 1)
    ).astype(jnp.float32)
    scales, current = [], []
    for gram in grams:
        square_sum = jnp.sum(gram * eye, keepdims=True)
        scale = 1.0 / (jnp.sqrt(square_sum) + 1e-07)
        scales.append(scale)
        current.append(gram * scale * scale)
    totals = None
    for number in range(ITERS):
        split = [halves(gram) for gram in current]
        squares = [product(gram, gram) for gram in split]
        steps = [
            COEF_A * eye + COEF_B * gram + COEF_C * square for gram, square in zip(current, squares)
        ]
        step_split = [halves(step) for step in steps]
        if totals is None:
            totals_next = steps
        else:
            total_split = [halves(total) for total in totals]
            totals_next = [product(s, t) for s, t in zip(step_split, total_split)]
        if number < ITERS - 1:
            half = [halves(product(s, g)) for s, g in zip(step_split, split)]
            current = [product(h, s) for h, s in zip(half, step_split)]
        totals = totals_next
    factor = 0.2 * math.sqrt(width)
    return [total * (scale * factor) for total, scale in zip(totals, scales)]


class Copies:
    def __init__(self, sems):
        self.sems, self.count = sems, 0

    def start(self, source, target):
        copy = pltpu.make_async_copy(source, target, self.sems.at[self.count])
        copy.start()
        self.count += 1
        return copy


def start_tokens(copies, pieces, spans, tokens, offset=0):
    started = []
    for piece, (begin, count) in zip(pieces, spans):
        target = tokens.at[pl.ds(offset, count)]
        started.append(copies.start(piece.at[pl.ds(begin, count)], target))
        offset += count
    return started


def start_upstream(copies, place_ref, first_block, upstream_ref, upstream):
    started = []
    for block in range(upstream.shape[0] // BLOCK):
        begin = pl.multiple_of(place_ref[first_block + block] * BLOCK, BLOCK)
        target = upstream.at[pl.ds(block * BLOCK, BLOCK)]
        started.append(copies.start(upstream_ref.at[pl.ds(begin, BLOCK)], target))
    return started


def wait_all(copies):
    for copy in copies:
        copy.wait()


def head_gradient(queries, scaled):
    inverse = lax.rsqrt(jnp.mean(queries * queries, axis=0, keepdims=True) + 1e-06)
    normed = queries * inverse
    projection = jnp.mean(normed * scaled, axis=0, keepdims=True)
    return (scaled - normed * projection) * inverse


def rotated_gradient(
    place_ref, first_block, gain_ref, ids_ref, tokens, weight, upstream, turned, rotated, base, ready
):
    rows = upstream.shape[0]
    size = gain_ref.shape[1]
    heads = weight.shape[0] // size
    gain = jnp.broadcast_to(gain_ref[...], (BLOCK, size)).T
    for block in range(rows // BLOCK):
        span = slice(block * BLOCK, (block + 1) * BLOCK)
        for head in range(heads):
            columns = slice(head * size, (head + 1) * size)
            turned[columns, span] = gain * upstream[span, columns].astype(jnp.float32).T
    live = []
    for block in range(rows // BLOCK):
        ids = ids_ref[pl.ds(place_ref[first_block + block], 1), :]
        live.append((ids != 0).astype(jnp.float32))
    live = jnp.concatenate(live, 1)
    wait_all(ready)
    for begin in range(0, rows, 2 * BLOCK):
        count = min(2 * BLOCK, rows - begin)
        span = pl.ds(base + begin, count)
        there = slice(begin, begin + count)
        queries = contract(weight[...], tokens[span, :], 1, 1)
        for head in range(heads):
            columns = slice(head * size, (head + 1) * size)
            grad = head_gradient(queries[columns], turned[columns, there])
            rotated[columns, span] = (grad * live[:, there]).astype(jnp.bfloat16)


def early_kernel(first_block, spans, *refs):
    count = len(spans)
    place_ref, gain_ref, ids_ref, upstream_ref, weight = refs[:5]
    pieces, refs = refs[5 : 5 + count], refs[5 + count :]
    _, out_ref, _, tokens, upstream, turned, rotated, sems = refs
    copies = Copies(sems)
    needed = start_upstream(copies, place_ref, first_block, upstream_ref, upstream)
    ready = start_tokens(copies, pieces, spans, tokens)
    wait_all(needed)
    rotated_gradient(
        place_ref, first_block, gain_ref, ids_ref, tokens, weight, upstream, turned, rotated, 0, ready
    )

    @pl.loop(0, out_ref.shape[1] // TILE)
    def _(tile):
        columns = pl.ds(pl.multiple_of(tile * TILE, TILE), TILE)
        out_ref[:, columns] = contract(rotated[...], tokens[:, columns], 1, 0)


def late_kernel(first_block, spans, *refs):
    count = len(spans)
    place_ref, gain_ref, ids_ref, upstream_ref, weight, before = refs[:6]
    pieces, refs = refs[6 : 6 + count], refs[6 + count :]
    out_ref, tokens, upstream, turned, rotated, sems = refs
    copies = Copies(sems)
    needed = start_upstream(copies, place_ref, first_block, upstream_ref, upstream)
    ready = start_tokens(copies, pieces, spans, tokens)
    wait_all(needed)
    rotated_gradient(
        place_ref, first_block, gain_ref, ids_ref, tokens, weight, upstream, turned, rotated, 0, ready
    )

    @pl.loop(0, out_ref.shape[1] // TILE)
    def _(tile):
        columns = pl.ds(pl.multiple_of(tile * TILE, TILE), TILE)
        out_ref[:, columns] = before[:, columns] + contract(rotated[...], tokens[:, columns], 1, 0)


def renew_kernel(first_block, count, *refs):
    place_ref, gain_ref, ids_ref, upstream_ref, weight, before_ref = refs[:6]
    refs = refs[6:]
    pieces, (mine_ref, theirs_ref) = refs[:count], refs[count : count + 2]
    tokens, upstream, turned, rotated, split, factors, sems = refs[count + 2 :]
    all_rows, width = weight.shape
    size = gain_ref.shape[1]
    heads = all_rows // size
    tiles = width // TILE
    copies = Copies(sems)
    needed = start_upstream(copies, place_ref, first_block, upstream_ref, upstream)
    offset = 0
    for piece in pieces:
        tokens[pl.ds(offset, piece.shape[0]), :] = piece[...]
        offset += piece.shape[0]
    wait_all(needed)
    rotated_gradient(
        place_ref, first_block, gain_ref, ids_ref, tokens, weight, upstream, turned, rotated, 0, []
    )

    @pl.loop(0, tiles)
    def _(tile):
        columns = pl.ds(pl.multiple_of(tile * TILE, TILE), TILE)
        part = contract(rotated[...], tokens[:, columns], 1, 0) + before_ref[:, columns]
        high, low = halves(part)
        for head in range(heads):
            span = slice(head * size, (head + 1) * size)
            split[head, :size, columns] = high[span]
            split[head, size:, columns] = low[span]

    grams = []
    for head in range(heads):
        both = split[head]
        whole = contract(both, both, 1, 1)
        grams.append(
            whole[:size, :size] + whole[:size, size:] + whole[size:, :size] + whole[size:, size:]
        )
    for head, factor in enumerate(orthogonal_factors(grams, width)):
        high, low = halves(factor)
        factors[head, :size, :size] = high
        factors[head, :size, size:] = high
        factors[head, size:, :size] = low
        factors[head, size:, size:] = jnp.zeros_like(low)

    core_is_zero = place_ref[10] == 0
    indices = []
    for chip in range(8):
        step_y = lax.rem(chip // 2 - place_ref[8] + 4, 4)
        step_z = lax.rem(chip % 2 - place_ref[9] + 2, 2)
        indices.append(step_y * 2 + step_z)

    @pl.loop(0, tiles)
    def _(tile):
        columns = pl.ds(pl.multiple_of(tile * TILE, TILE), TILE)
        for pair in range(heads // 2):
            renewed = []
            for head in (2 * pair, 2 * pair + 1):
                both = contract(factors[head], split[head, :, columns], 1, 0)
                change = both[:size] + both[size:]
                old = weight[head * size : (head + 1) * size, columns].astype(jnp.float32)
                renewed.append(old - change)
            span = pl.ds(pair * 16, 16)
            for chip, index in enumerate(indices):
                parts = []
                for core in range(2):
                    begin = (chip * 2 + core) * 8
                    parts.append(
                        jnp.concatenate([value[begin : begin + 8] for value in renewed], 0)
                    )
                mine = jnp.where(core_is_zero, parts[0], parts[1])
                theirs = jnp.where(core_is_zero, parts[1], parts[0])
                mine_ref[index, span, columns] = mine.astype(jnp.bfloat16)
                theirs_ref[index, span, columns] = theirs.astype(jnp.bfloat16)


OUTSIDE = pl.BlockSpec(memory_space=pltpu.HBM)
INSIDE = pl.BlockSpec(memory_space=pltpu.VMEM)
SCALARS = pl.BlockSpec(memory_space=pltpu.SMEM)


def outside(array):
    return pltpu.with_memory_space_constraint(array, pltpu.HBM)


def call(kernel, out_shape, in_specs, out_specs, scratch, flops, moved, vmem, operands, aliases=None):
    return pl.pallas_call(
        kernel,
        out_shape=out_shape,
        in_specs=in_specs,
        out_specs=out_specs,
        scratch_shapes=scratch,
        input_output_aliases=aliases or {},
        compiler_params=pltpu.CompilerParams(vmem_limit_bytes=vmem * 1024 * 1024),
        cost_estimate=pl.CostEstimate(flops=flops, bytes_accessed=moved, transcendentals=0),
    )(*operands)


def scratch_of(common, rows):
    all_rows, width = common[-1].shape
    return [
        pltpu.VMEM((rows, all_rows), jnp.bfloat16),
        pltpu.VMEM((all_rows, rows), jnp.float32),
    ]


def arrays_of(pieces):
    return [outside(piece[0] if isinstance(piece, tuple) else piece) for piece in pieces]


def spans_of(pieces):
    return [piece[1:] if isinstance(piece, tuple) else (0, piece.shape[0]) for piece in pieces]


def rows_of(pieces):
    return sum(count for _, count in spans_of(pieces))


COMMON_SPECS = [SCALARS, INSIDE, INSIDE, OUTSIDE, INSIDE]


def pick_kernel(picks, count, *refs):
    sources, targets, sems = refs[:count], refs[-1 - len(picks) : -1], refs[-1]
    copies = Copies(sems)
    started = []
    for target, parts in zip(targets, picks):
        offset = 0
        for number, begin, rows in parts:
            source = sources[number].at[pl.ds(begin, rows)]
            started.append(copies.start(source, target.at[pl.ds(offset, rows)]))
            offset += rows
    wait_all(started)


def pick_call(arrays, picks):
    shapes = []
    for parts in picks:
        rows = sum(part[2] for part in parts)
        shapes.append(jax.ShapeDtypeStruct((rows, arrays[0].shape[1]), arrays[0].dtype))
    moved = 4 * sum(shape.size for shape in shapes)
    scratch = [pltpu.SemaphoreType.DMA((sum(len(parts) for parts in picks),))]
    return call(
        functools.partial(pick_kernel, picks, len(arrays)),
        tuple(shapes),
        [OUTSIDE] * len(arrays),
        (INSIDE,) * len(shapes),
        scratch,
        0,
        moved,
        PICK_VMEM,
        list(map(outside, arrays)),
    )


def early_call(common, first_block, pieces, passed):
    all_rows, width = common[-1].shape
    rows = rows_of(pieces)
    return call(
        functools.partial(early_kernel, first_block, spans_of(pieces)),
        (
            jax.ShapeDtypeStruct((all_rows, width), jnp.float32),
            jax.ShapeDtypeStruct(passed.shape, passed.dtype),
        ),
        COMMON_SPECS + [OUTSIDE] * (len(pieces) + 1),
        (INSIDE, OUTSIDE),
        [pltpu.VMEM((rows, width), jnp.bfloat16)]
        + scratch_of(common, rows)
        + [
            pltpu.VMEM((all_rows, rows), jnp.bfloat16),
            pltpu.SemaphoreType.DMA((len(pieces) + rows // BLOCK,)),
        ],
        4 * rows * all_rows * width,
        (6 * all_rows + 2 * rows) * width,
        EARLY_VMEM,
        [*common, *arrays_of(pieces), passed],
        {len(common) + len(pieces): 1},
    )


def late_call(common, first_block, before, pieces):
    all_rows, width = common[-1].shape
    rows = rows_of(pieces)
    return call(
        functools.partial(late_kernel, first_block, spans_of(pieces)),
        jax.ShapeDtypeStruct(before.shape, before.dtype),
        COMMON_SPECS + [INSIDE] + [OUTSIDE] * len(pieces),
        INSIDE,
        [pltpu.VMEM((rows, width), jnp.bfloat16)]
        + scratch_of(common, rows)
        + [
            pltpu.VMEM((all_rows, rows), jnp.bfloat16),
            pltpu.SemaphoreType.DMA((len(pieces) + rows // BLOCK,)),
        ],
        4 * rows * all_rows * width,
        2 * (rows + all_rows) * width,
        LATE_VMEM,
        [*common, before, *arrays_of(pieces)],
        {len(common): 0},
    )


def renew_call(common, first_block, before, pieces):
    all_rows, width = common[-1].shape
    size = common[1].shape[1]
    heads = all_rows // size
    rows = rows_of(pieces)
    shape = jax.ShapeDtypeStruct((8, all_rows // 16, width), jnp.bfloat16)
    return call(
        functools.partial(renew_kernel, first_block, len(pieces)),
        (shape, shape),
        COMMON_SPECS + [INSIDE] * (1 + len(pieces)),
        (INSIDE, INSIDE),
        [pltpu.VMEM((rows, width), jnp.bfloat16)]
        + scratch_of(common, rows)
        + [
            pltpu.VMEM((all_rows, rows), jnp.bfloat16),
            pltpu.VMEM((heads, 2 * size, width), jnp.bfloat16),
            pltpu.VMEM((heads, 2 * size, 2 * size), jnp.bfloat16),
            pltpu.SemaphoreType.DMA((rows // BLOCK,)),
        ],
        (4 * rows + 16 * size) * all_rows * width,
        8 * all_rows * width,
        RENEW_VMEM,
        [*common, before, *pieces],
    )


def shards(
    activations,
    token_ids,
    cotangent,
    inner_weight,
    query_gain,
    outer_weight,
    momentum,
    average_weight,
):
    weights = inner_weight[0]
    head_count, head_size, model_width = weights.shape
    flat_weight = weights.reshape(head_count * head_size, model_width)

    place = lax.axis_index("grp")
    spot = lax.axis_index("rep")
    numbers = []
    for step_z, step_x in ((0, 0), (0, -1), (0, 1), (1, 0), (1, -1), (1, 1), (0, 2), (1, 2)):
        numbers.append(((place // RING + step_z) % 2) * RING + (place + step_x) % RING)
    numbers += [spot // 4, (spot // 2) % 2, spot % 2]
    common = (
        jnp.stack(numbers).astype(jnp.int32),
        query_gain[None, :],
        token_ids.reshape(2 * RING, BLOCK),
        outside(cotangent),
        flat_weight,
    )

    rows_b = BLOCK - ROWS_A
    left, right = along_x(activations, 1), along_x(activations, -1)
    own_a, own_b = pick_call([activations], [[(0, 0, ROWS_A)], [(0, ROWS_A, rows_b)]])
    over_a = across_z(own_a)
    over_left_a, over_right_a = along_x(over_a, 1), along_x(over_a, -1)
    over_b = across_z(own_b)
    left_far, right_far, right_b, sides_b = pick_call(
        [left, right],
        [
            [(0, 0, FAR)],
            [(1, FAR, ROWS_A - FAR)],
            [(1, ROWS_A, rows_b)],
            [(0, ROWS_A, rows_b), (1, ROWS_A, rows_b)],
        ],
    )
    far_b = along_x(right_b, -1)
    far0 = along_x(left_far, 1)
    over_b2 = across_z(sides_b)
    before, right_far = early_call(common, 0, [activations, left, right, over_a, over_b], right_far)
    over_left_far, over_right_far, right_far = pick_call(
        [over_left_a, over_right_a, right_far],
        [[(0, 0, FAR_A)], [(1, FAR_A, ROWS_A - FAR_A)], [(2, 0, ROWS_A - FAR)]],
    )
    over_far0, over_far1 = along_x(over_left_far, 1), along_x(over_right_far, -1)
    far1 = along_x(right_far, -1)
    over_far_b = across_z(far_b)
    late = [over_left_a, (over_b2, 0, rows_b), over_right_a, (over_b2, rows_b, rows_b)]
    before = late_call(common, 4, before, late)
    last = [far0, far1, far_b, over_far0, over_far1, over_far_b]
    mine, theirs = renew_call(common, 6, before, last)

    theirs = to_other_core(theirs)
    summed = None
    for step_y, step_z in ((2, 1), (3, 1), (1, 0), (3, 0), (0, 1), (1, 1), (2, 0), (0, 0)):
        index = step_y * 2 + step_z
        pair = mine[index].astype(jnp.float32) + theirs[index].astype(jnp.float32)
        if index:
            pair = to_chip(pair.astype(jnp.bfloat16), step_y, step_z).astype(jnp.float32)
        summed = pair if summed is None else summed + pair
    summed = summed.reshape(outer_weight.shape)

    mean_weight = summed / lax.axis_size("rep")
    pseudo = outer_weight - mean_weight
    new_momentum = 0.9 * momentum + pseudo
    new_outer = outer_weight - 0.7 * (pseudo + 0.9 * new_momentum)
    new_average = 0.9 * average_weight + 0.1 * new_outer
    return (new_outer, new_momentum, new_average)


def solution(mesh):
    placed = (
        P(("rep", "grp"), None),
        P("rep"),
        P("rep", "grp"),
        P("rep", "grp", None, None),
        P(),
        P("grp", "rep", None),
        P("grp", "rep", None),
        P("grp", "rep", None),
    )
    return jax.shard_map(
        shards,
        mesh=mesh,
        in_specs=placed,
        out_specs=(P("grp", "rep", None), P("grp", "rep", None), P("grp", "rep", None)),
        check_vma=False,
    )
```

```python
import functools
import math

import jax
import jax.numpy as jnp
from jax import lax
from jax.experimental import pallas as pl
from jax.experimental.pallas import tpu as pltpu
from jax.sharding import PartitionSpec as P

ITERS = 5
COEF_A = 3.4445
COEF_B = -4.775
COEF_C = 2.0315

RING = 4
BLOCK = 128
ROWS_A = 80
FAR = 16
TILE = 2560
EARLY_VMEM, LATE_VMEM, RENEW_VMEM, PICK_VMEM, MINE_VMEM = 18, 12, 16, 8, 8


def along_x(array, step):
    pairs = [(z * RING + x, z * RING + (x + step) % RING) for z in range(2) for x in range(RING)]
    return lax.ppermute(array, "grp", pairs)


def across_z(array):
    return lax.ppermute(array, "grp", [(g, (g + RING) % (2 * RING)) for g in range(2 * RING)])


def to_other_core(array):
    return lax.ppermute(array, "rep", [(r, r ^ 1) for r in range(16)])


def to_chip(array, step_y, step_z):
    pairs = []
    for y in range(4):
        for z in range(2):
            for core in range(2):
                source = (y * 2 + z) * 2 + core
                target = (((y + step_y) % 4) * 2 + (z + step_z) % 2) * 2 + core
                pairs.append((source, target))
    return lax.ppermute(array, "rep", pairs)


def contract(left, right, left_dim, right_dim):
    return lax.dot_general(
        left, right, (((left_dim,), (right_dim,)), ((), ())), preferred_element_type=jnp.float32
    )


def halves(value):
    high = value.astype(jnp.bfloat16)
    return high, (value - high.astype(jnp.float32)).astype(jnp.bfloat16)


def product(left, right):
    high, low = left
    right_high, right_low = right
    wide = contract(
        jnp.concatenate([high, low], 1), jnp.concatenate([right_high, right_high], 0), 1, 0
    )
    return wide + contract(high, right_low, 1, 0)


def orthogonal_factors(grams, width):
    size = grams[0].shape[0]
    eye = (
        lax.broadcasted_iota(jnp.int32, (size, size), 0)
        == lax.broadcasted_iota(jnp.int32, (size, size), 1)
    ).astype(jnp.float32)
    scales, current = [], []
    for gram in grams:
        square_sum = jnp.sum(gram * eye, keepdims=True)
        scale = 1.0 / (jnp.sqrt(square_sum) + 1e-07)
        scales.append(scale)
        current.append(gram * scale * scale)
    totals = None
    for number in range(ITERS):
        split = [halves(gram) for gram in current]
        squares = [product(gram, gram) for gram in split]
        steps = [
            COEF_A * eye + COEF_B * gram + COEF_C * square for gram, square in zip(current, squares)
        ]
        step_split = [halves(step) for step in steps]
        if totals is None:
            totals_next = steps
        else:
            total_split = [halves(total) for total in totals]
            totals_next = [product(s, t) for s, t in zip(step_split, total_split)]
        if number < ITERS - 1:
            half = [halves(product(s, g)) for s, g in zip(step_split, split)]
            current = [product(h, s) for h, s in zip(half, step_split)]
        totals = totals_next
    factor = 0.2 * math.sqrt(width)
    return [total * (scale * factor) for total, scale in zip(totals, scales)]


class Copies:
    def __init__(self, sems):
        self.sems, self.count = sems, 0

    def start(self, source, target):
        copy = pltpu.make_async_copy(source, target, self.sems.at[self.count])
        copy.start()
        self.count += 1
        return copy


def start_tokens(copies, pieces, spans, tokens, offset=0):
    started = []
    for piece, (begin, count) in zip(pieces, spans):
        target = tokens.at[pl.ds(offset, count)]
        started.append(copies.start(piece.at[pl.ds(begin, count)], target))
        offset += count
    return started


def start_upstream(copies, place_ref, first_block, upstream_ref, upstream):
    started = []
    for block in range(upstream.shape[0] // BLOCK):
        begin = pl.multiple_of(place_ref[first_block + block] * BLOCK, BLOCK)
        target = upstream.at[pl.ds(block * BLOCK, BLOCK)]
        started.append(copies.start(upstream_ref.at[pl.ds(begin, BLOCK)], target))
    return started


def wait_all(copies):
    for copy in copies:
        copy.wait()


def head_gradient(queries, scaled):
    inverse = lax.rsqrt(jnp.mean(queries * queries, axis=0, keepdims=True) + 1e-06)
    normed = queries * inverse
    projection = jnp.mean(normed * scaled, axis=0, keepdims=True)
    return (scaled - normed * projection) * inverse


def rotated_gradient(
    place_ref, first_block, gain_ref, ids_ref, tokens, weight, upstream, turned, rotated, base, ready
):
    rows = upstream.shape[0]
    size = gain_ref.shape[1]
    heads = weight.shape[0] // size
    gain = jnp.broadcast_to(gain_ref[...], (BLOCK, size)).T
    for block in range(rows // BLOCK):
        span = slice(block * BLOCK, (block + 1) * BLOCK)
        for head in range(heads):
            columns = slice(head * size, (head + 1) * size)
            turned[columns, span] = gain * upstream[span, columns].astype(jnp.float32).T
    live = []
    for block in range(rows // BLOCK):
        ids = ids_ref[pl.ds(place_ref[first_block + block], 1), :]
        live.append((ids != 0).astype(jnp.float32))
    live = jnp.concatenate(live, 1)
    wait_all(ready)
    for begin in range(0, rows, 2 * BLOCK):
        count = min(2 * BLOCK, rows - begin)
        span = pl.ds(base + begin, count)
        there = slice(begin, begin + count)
        queries = contract(weight[...], tokens[span, :], 1, 1)
        for head in range(heads):
            columns = slice(head * size, (head + 1) * size)
            grad = head_gradient(queries[columns], turned[columns, there])
            rotated[columns, span] = (grad * live[:, there]).astype(jnp.bfloat16)


def early_kernel(first_block, spans, *refs):
    count = len(spans)
    place_ref, gain_ref, ids_ref, upstream_ref, weight = refs[:5]
    pieces, refs = refs[5 : 5 + count], refs[5 + count :]
    out_ref, tokens, upstream, turned, rotated, sems = refs
    copies = Copies(sems)
    needed = start_upstream(copies, place_ref, first_block, upstream_ref, upstream)
    ready = start_tokens(copies, pieces, spans, tokens)
    wait_all(needed)
    rotated_gradient(
        place_ref, first_block, gain_ref, ids_ref, tokens, weight, upstream, turned, rotated, 0, ready
    )

    @pl.loop(0, out_ref.shape[1] // TILE)
    def _(tile):
        columns = pl.ds(pl.multiple_of(tile * TILE, TILE), TILE)
        out_ref[:, columns] = contract(rotated[...], tokens[:, columns], 1, 0)


def late_kernel(first_block, spans, *refs):
    count = len(spans)
    place_ref, gain_ref, ids_ref, upstream_ref, weight, before = refs[:6]
    pieces, refs = refs[6 : 6 + count], refs[6 + count :]
    out_ref, tokens, upstream, turned, rotated, sems = refs
    copies = Copies(sems)
    needed = start_upstream(copies, place_ref, first_block, upstream_ref, upstream)
    ready = start_tokens(copies, pieces, spans, tokens)
    wait_all(needed)
    rotated_gradient(
        place_ref, first_block, gain_ref, ids_ref, tokens, weight, upstream, turned, rotated, 0, ready
    )

    @pl.loop(0, out_ref.shape[1] // TILE)
    def _(tile):
        columns = pl.ds(pl.multiple_of(tile * TILE, TILE), TILE)
        out_ref[:, columns] = before[:, columns] + contract(rotated[...], tokens[:, columns], 1, 0)


def renew_kernel(first_block, count, *refs):
    place_ref, gain_ref, ids_ref, upstream_ref, weight, before_ref = refs[:6]
    refs = refs[6:]
    pieces, (theirs_ref, split, factors) = refs[:count], refs[count : count + 3]
    tokens, upstream, turned, rotated, sems = refs[count + 3 :]
    all_rows, width = weight.shape
    size = gain_ref.shape[1]
    heads = all_rows // size
    tiles = width // TILE
    copies = Copies(sems)
    needed = start_upstream(copies, place_ref, first_block, upstream_ref, upstream)
    offset = 0
    for piece in pieces:
        tokens[pl.ds(offset, piece.shape[0]), :] = piece[...]
        offset += piece.shape[0]
    wait_all(needed)
    rotated_gradient(
        place_ref, first_block, gain_ref, ids_ref, tokens, weight, upstream, turned, rotated, 0, []
    )

    @pl.loop(0, tiles)
    def _(tile):
        columns = pl.ds(pl.multiple_of(tile * TILE, TILE), TILE)
        part = contract(rotated[...], tokens[:, columns], 1, 0) + before_ref[:, columns]
        high, low = halves(part)
        for head in range(heads):
            span = slice(head * size, (head + 1) * size)
            split[head, :size, columns] = high[span]
            split[head, size:, columns] = low[span]

    grams = []
    for head in range(heads):
        both = split[head]
        whole = contract(both, both, 1, 1)
        grams.append(
            whole[:size, :size] + whole[:size, size:] + whole[size:, :size] + whole[size:, size:]
        )
    core_is_zero = place_ref[10] == 0
    for head, factor in enumerate(orthogonal_factors(grams, width)):
        for which in range(2):
            high, low = halves(rows_of_core(factor, core_is_zero, which))
            half = high.shape[0]
            factors[head, which, :half, :size] = high
            factors[head, which, :half, size:] = high
            factors[head, which, half:, :size] = low
            factors[head, which, half:, size:] = jnp.zeros_like(low)
    change_rows(place_ref, weight, split, factors, theirs_ref, 1)


def rows_of_core(value, core_is_zero, which):
    rows = []
    for begin in range(0, value.shape[0], 16):
        first, second = value[begin : begin + 8], value[begin + 8 : begin + 16]
        if which:
            first, second = second, first
        rows.append(jnp.where(core_is_zero, first, second))
    return jnp.concatenate(rows, 0)


def change_rows(place_ref, weight, split, factors, out_ref, which):
    all_rows, width = weight.shape
    heads = split.shape[0]
    size = all_rows // heads
    core_is_zero = place_ref[10] == 0
    indices = []
    for chip in range(8):
        step_y = lax.rem(chip // 2 - place_ref[8] + 4, 4)
        step_z = lax.rem(chip % 2 - place_ref[9] + 2, 2)
        indices.append(step_y * 2 + step_z)

    @pl.loop(0, width // TILE)
    def _(tile):
        columns = pl.ds(pl.multiple_of(tile * TILE, TILE), TILE)
        for pair in range(heads // 2):
            renewed = []
            for head in (2 * pair, 2 * pair + 1):
                both = contract(factors[head, which], split[head, :, columns], 1, 0)
                change = both[: size // 2] + both[size // 2 :]
                old = weight[head * size : (head + 1) * size, columns].astype(jnp.float32)
                renewed.append(rows_of_core(old, core_is_zero, which) - change)
            span = pl.ds(pair * 16, 16)
            for chip, index in enumerate(indices):
                rows = [value[chip * 8 : chip * 8 + 8] for value in renewed]
                out_ref[index, span, columns] = jnp.concatenate(rows, 0).astype(jnp.bfloat16)


def mine_kernel(place_ref, weight, split, factors, mine_ref):
    change_rows(place_ref, weight, split, factors, mine_ref, 0)


OUTSIDE = pl.BlockSpec(memory_space=pltpu.HBM)
INSIDE = pl.BlockSpec(memory_space=pltpu.VMEM)
SCALARS = pl.BlockSpec(memory_space=pltpu.SMEM)


def outside(array):
    return pltpu.with_memory_space_constraint(array, pltpu.HBM)


def call(kernel, out_shape, in_specs, out_specs, scratch, flops, moved, vmem, operands, aliases=None):
    return pl.pallas_call(
        kernel,
        out_shape=out_shape,
        in_specs=in_specs,
        out_specs=out_specs,
        scratch_shapes=scratch,
        input_output_aliases=aliases or {},
        compiler_params=pltpu.CompilerParams(vmem_limit_bytes=vmem * 1024 * 1024),
        cost_estimate=pl.CostEstimate(flops=flops, bytes_accessed=moved, transcendentals=0),
    )(*operands)


def scratch_of(common, rows):
    all_rows, width = common[-1].shape
    return [
        pltpu.VMEM((rows, all_rows), jnp.bfloat16),
        pltpu.VMEM((all_rows, rows), jnp.float32),
    ]


def arrays_of(pieces):
    return [outside(piece[0] if isinstance(piece, tuple) else piece) for piece in pieces]


def spans_of(pieces):
    return [piece[1:] if isinstance(piece, tuple) else (0, piece.shape[0]) for piece in pieces]


def rows_of(pieces):
    return sum(count for _, count in spans_of(pieces))


COMMON_SPECS = [SCALARS, INSIDE, INSIDE, OUTSIDE, INSIDE]


def pick_kernel(picks, count, *refs):
    sources, targets, sems = refs[:count], refs[-1 - len(picks) : -1], refs[-1]
    copies = Copies(sems)
    started = []
    for target, parts in zip(targets, picks):
        offset = 0
        for number, begin, rows in parts:
            source = sources[number].at[pl.ds(begin, rows)]
            started.append(copies.start(source, target.at[pl.ds(offset, rows)]))
            offset += rows
    wait_all(started)


def pick_call(arrays, picks, after=()):
    shapes = []
    for parts in picks:
        rows = sum(part[2] for part in parts)
        shapes.append(jax.ShapeDtypeStruct((rows, arrays[0].shape[1]), arrays[0].dtype))
    moved = 4 * sum(shape.size for shape in shapes)
    scratch = [pltpu.SemaphoreType.DMA((sum(len(parts) for parts in picks),))]
    return call(
        functools.partial(pick_kernel, picks, len(arrays)),
        tuple(shapes),
        [OUTSIDE] * (len(arrays) + len(after)),
        (INSIDE,) * len(shapes),
        scratch,
        0,
        moved,
        PICK_VMEM,
        [*map(outside, arrays), *after],
    )


def early_call(common, first_block, pieces):
    all_rows, width = common[-1].shape
    rows = rows_of(pieces)
    return call(
        functools.partial(early_kernel, first_block, spans_of(pieces)),
        jax.ShapeDtypeStruct((all_rows, width), jnp.float32),
        COMMON_SPECS + [OUTSIDE] * len(pieces),
        INSIDE,
        [pltpu.VMEM((rows, width), jnp.bfloat16)]
        + scratch_of(common, rows)
        + [
            pltpu.VMEM((all_rows, rows), jnp.bfloat16),
            pltpu.SemaphoreType.DMA((len(pieces) + rows // BLOCK,)),
        ],
        4 * rows * all_rows * width,
        (6 * all_rows + 2 * rows) * width,
        EARLY_VMEM,
        [*common, *arrays_of(pieces)],
    )


def late_call(common, first_block, before, pieces):
    all_rows, width = common[-1].shape
    rows = rows_of(pieces)
    return call(
        functools.partial(late_kernel, first_block, spans_of(pieces)),
        jax.ShapeDtypeStruct(before.shape, before.dtype),
        COMMON_SPECS + [INSIDE] + [OUTSIDE] * len(pieces),
        INSIDE,
        [pltpu.VMEM((rows, width), jnp.bfloat16)]
        + scratch_of(common, rows)
        + [
            pltpu.VMEM((all_rows, rows), jnp.bfloat16),
            pltpu.SemaphoreType.DMA((len(pieces) + rows // BLOCK,)),
        ],
        4 * rows * all_rows * width,
        2 * (rows + all_rows) * width,
        LATE_VMEM,
        [*common, before, *arrays_of(pieces)],
        {len(common): 0},
    )


def renew_call(common, first_block, before, pieces):
    all_rows, width = common[-1].shape
    size = common[1].shape[1]
    heads = all_rows // size
    rows = rows_of(pieces)
    shape = jax.ShapeDtypeStruct((8, all_rows // 16, width), jnp.bfloat16)
    return call(
        functools.partial(renew_kernel, first_block, len(pieces)),
        (
            shape,
            jax.ShapeDtypeStruct((heads, 2 * size, width), jnp.bfloat16),
            jax.ShapeDtypeStruct((heads, 2, size, 2 * size), jnp.bfloat16),
        ),
        COMMON_SPECS + [INSIDE] * (1 + len(pieces)),
        (INSIDE, INSIDE, INSIDE),
        [pltpu.VMEM((rows, width), jnp.bfloat16)]
        + scratch_of(common, rows)
        + [
            pltpu.VMEM((all_rows, rows), jnp.bfloat16),
            pltpu.SemaphoreType.DMA((rows // BLOCK,)),
        ],
        (4 * rows + 16 * size) * all_rows * width,
        8 * all_rows * width,
        RENEW_VMEM,
        [*common, before, *pieces],
    )


def mine_call(common, split, factors, shape):
    all_rows, width = common[-1].shape
    return call(
        mine_kernel,
        jax.ShapeDtypeStruct(shape, jnp.bfloat16),
        [SCALARS, INSIDE, INSIDE, INSIDE],
        INSIDE,
        [],
        4 * all_rows * split.shape[1] * width,
        4 * all_rows * width,
        MINE_VMEM,
        [common[0], common[-1], split, factors],
    )


def shards(
    activations,
    token_ids,
    cotangent,
    inner_weight,
    query_gain,
    outer_weight,
    momentum,
    average_weight,
):
    weights = inner_weight[0]
    head_count, head_size, model_width = weights.shape
    flat_weight = weights.reshape(head_count * head_size, model_width)

    place = lax.axis_index("grp")
    spot = lax.axis_index("rep")
    numbers = []
    for step_z, step_x in ((0, 0), (0, -1), (0, 1), (1, 0), (1, -1), (1, 1), (0, 2), (1, 2)):
        numbers.append(((place // RING + step_z) % 2) * RING + (place + step_x) % RING)
    numbers += [spot // 4, (spot // 2) % 2, spot % 2]
    common = (
        jnp.stack(numbers).astype(jnp.int32),
        query_gain[None, :],
        token_ids.reshape(2 * RING, BLOCK),
        outside(cotangent),
        flat_weight,
    )

    rows_b = BLOCK - ROWS_A
    left, right = along_x(activations, 1), along_x(activations, -1)
    own_a, own_b = pick_call([activations], [[(0, 0, ROWS_A)], [(0, ROWS_A, rows_b)]])
    over_a = across_z(own_a)
    over_left_a, over_right_a = along_x(over_a, 1), along_x(over_a, -1)
    over_b = across_z(own_b)
    left_far, right_b, sides_b = pick_call(
        [left, right],
        [
            [(0, 0, ROWS_A)],
            [(1, ROWS_A, rows_b)],
            [(0, ROWS_A, rows_b), (1, ROWS_A, rows_b)],
        ],
    )
    far_b = along_x(right_b, -1)
    far_a = along_x(left_far, 1)
    over_b2 = across_z(sides_b)
    before = early_call(common, 0, [activations, left, right, over_a, over_b])
    over_left_far, over_right_far = pick_call(
        [over_left_a, over_right_a], [[(0, 0, FAR)], [(1, FAR, ROWS_A - FAR)]], [before]
    )
    over_far0, over_far1 = along_x(over_left_far, 1), along_x(over_right_far, -1)
    over_far_b = across_z(far_b)
    late = [over_left_a, (over_b2, 0, rows_b), over_right_a, (over_b2, rows_b, rows_b)]
    before = late_call(common, 4, before, late)
    last = [far_a, far_b, over_far0, over_far1, over_far_b]
    theirs, split, factors = renew_call(common, 6, before, last)
    mine = mine_call(common, split, factors, theirs.shape)

    theirs = to_other_core(theirs)
    summed = None
    for step_y, step_z in ((2, 1), (3, 1), (1, 0), (3, 0), (0, 1), (1, 1), (2, 0), (0, 0)):
        index = step_y * 2 + step_z
        pair = mine[index].astype(jnp.float32) + theirs[index].astype(jnp.float32)
        if index:
            pair = to_chip(pair.astype(jnp.bfloat16), step_y, step_z).astype(jnp.float32)
        summed = pair if summed is None else summed + pair
    summed = summed.reshape(outer_weight.shape)

    mean_weight = summed / lax.axis_size("rep")
    pseudo = outer_weight - mean_weight
    new_momentum = 0.9 * momentum + pseudo
    new_outer = outer_weight - 0.7 * (pseudo + 0.9 * new_momentum)
    new_average = 0.9 * average_weight + 0.1 * new_outer
    return (new_outer, new_momentum, new_average)


def solution(mesh):
    placed = (
        P(("rep", "grp"), None),
        P("rep"),
        P("rep", "grp"),
        P("rep", "grp", None, None),
        P(),
        P("grp", "rep", None),
        P("grp", "rep", None),
        P("grp", "rep", None),
    )
    return jax.shard_map(
        shards,
        mesh=mesh,
        in_specs=placed,
        out_specs=(P("grp", "rep", None), P("grp", "rep", None), P("grp", "rep", None)),
        check_vma=False,
    )
```

```python
import functools
import math

import jax
import jax.numpy as jnp
from jax import lax
from jax.experimental import pallas as pl
from jax.experimental.pallas import tpu as pltpu
from jax.sharding import PartitionSpec as P

ITERS = 5
COEF_A = 3.4445
COEF_B = -4.775
COEF_C = 2.0315

RING = 4
BLOCK = 128
ROWS_A = 80
FAR = 16
TILE = 2560
EARLY_VMEM, LATE_VMEM, RENEW_VMEM, PICK_VMEM, MINE_VMEM = 18, 12, 16, 8, 8


def along_x(array, step):
    pairs = [(z * RING + x, z * RING + (x + step) % RING) for z in range(2) for x in range(RING)]
    return lax.ppermute(array, "grp", pairs)


def across_z(array):
    return lax.ppermute(array, "grp", [(g, (g + RING) % (2 * RING)) for g in range(2 * RING)])


def to_other_core(array):
    return lax.ppermute(array, "rep", [(r, r ^ 1) for r in range(16)])


def to_chip(array, step_y, step_z):
    pairs = []
    for y in range(4):
        for z in range(2):
            for core in range(2):
                source = (y * 2 + z) * 2 + core
                target = (((y + step_y) % 4) * 2 + (z + step_z) % 2) * 2 + core
                pairs.append((source, target))
    return lax.ppermute(array, "rep", pairs)


def contract(left, right, left_dim, right_dim):
    return lax.dot_general(
        left, right, (((left_dim,), (right_dim,)), ((), ())), preferred_element_type=jnp.float32
    )


def halves(value):
    high = value.astype(jnp.bfloat16)
    return high, (value - high.astype(jnp.float32)).astype(jnp.bfloat16)


def product(left, right):
    high, low = left
    right_high, right_low = right
    return contract(
        jnp.concatenate([high, low, high], 1),
        jnp.concatenate([right_high, right_high, right_low], 0),
        1,
        0,
    )


def orthogonal_factors(grams, width):
    size = grams[0].shape[0]
    eye = (
        lax.broadcasted_iota(jnp.int32, (size, size), 0)
        == lax.broadcasted_iota(jnp.int32, (size, size), 1)
    ).astype(jnp.float32)
    scales, current = [], []
    for gram in grams:
        square_sum = jnp.sum(gram * eye, keepdims=True)
        scale = 1.0 / (jnp.sqrt(square_sum) + 1e-07)
        scales.append(scale)
        current.append(gram * scale * scale)
    totals = None
    for number in range(ITERS):
        split = [halves(gram) for gram in current]
        squares = [product(gram, gram) for gram in split]
        steps = [
            COEF_A * eye + COEF_B * gram + COEF_C * square for gram, square in zip(current, squares)
        ]
        step_split = [halves(step) for step in steps]
        if totals is None:
            totals_next = steps
        else:
            total_split = [halves(total) for total in totals]
            totals_next = [product(s, t) for s, t in zip(step_split, total_split)]
        if number < ITERS - 1:
            half = [halves(product(s, g)) for s, g in zip(step_split, split)]
            current = [product(h, s) for h, s in zip(half, step_split)]
        totals = totals_next
    factor = 0.2 * math.sqrt(width)
    return [total * (scale * factor) for total, scale in zip(totals, scales)]


class Copies:
    def __init__(self, sems):
        self.sems, self.count = sems, 0

    def start(self, source, target):
        copy = pltpu.make_async_copy(source, target, self.sems.at[self.count])
        copy.start()
        self.count += 1
        return copy


def start_tokens(copies, pieces, spans, tokens, offset=0):
    started = []
    for piece, (begin, count) in zip(pieces, spans):
        target = tokens.at[pl.ds(offset, count)]
        started.append(copies.start(piece.at[pl.ds(begin, count)], target))
        offset += count
    return started


def start_upstream(copies, place_ref, first_block, upstream_ref, upstream):
    started = []
    for block in range(upstream.shape[0] // BLOCK):
        begin = pl.multiple_of(place_ref[first_block + block] * BLOCK, BLOCK)
        target = upstream.at[pl.ds(block * BLOCK, BLOCK)]
        started.append(copies.start(upstream_ref.at[pl.ds(begin, BLOCK)], target))
    return started


def wait_all(copies):
    for copy in copies:
        copy.wait()


def head_gradient(queries, scaled):
    inverse = lax.rsqrt(jnp.mean(queries * queries, axis=0, keepdims=True) + 1e-06)
    normed = queries * inverse
    projection = jnp.mean(normed * scaled, axis=0, keepdims=True)
    return (scaled - normed * projection) * inverse


def rotated_gradient(
    place_ref, first_block, gain_ref, ids_ref, tokens, weight, upstream, turned, rotated, base, ready
):
    rows = upstream.shape[0]
    size = gain_ref.shape[1]
    heads = weight.shape[0] // size
    gain = jnp.broadcast_to(gain_ref[...], (BLOCK, size)).T
    for block in range(rows // BLOCK):
        span = slice(block * BLOCK, (block + 1) * BLOCK)
        for head in range(heads):
            columns = slice(head * size, (head + 1) * size)
            turned[columns, span] = gain * upstream[span, columns].astype(jnp.float32).T
    live = []
    for block in range(rows // BLOCK):
        ids = ids_ref[pl.ds(place_ref[first_block + block], 1), :]
        live.append((ids != 0).astype(jnp.float32))
    live = jnp.concatenate(live, 1)
    wait_all(ready)
    for begin in range(0, rows, 2 * BLOCK):
        count = min(2 * BLOCK, rows - begin)
        span = pl.ds(base + begin, count)
        there = slice(begin, begin + count)
        queries = contract(weight[...], tokens[span, :], 1, 1)
        for head in range(heads):
            columns = slice(head * size, (head + 1) * size)
            grad = head_gradient(queries[columns], turned[columns, there])
            rotated[columns, span] = (grad * live[:, there]).astype(jnp.bfloat16)


def early_kernel(first_block, spans, *refs):
    count = len(spans)
    place_ref, gain_ref, ids_ref, upstream_ref, weight = refs[:5]
    pieces, refs = refs[5 : 5 + count], refs[5 + count :]
    out_ref, tokens, upstream, turned, rotated, sems = refs
    copies = Copies(sems)
    needed = start_upstream(copies, place_ref, first_block, upstream_ref, upstream)
    ready = start_tokens(copies, pieces, spans, tokens)
    wait_all(needed)
    rotated_gradient(
        place_ref, first_block, gain_ref, ids_ref, tokens, weight, upstream, turned, rotated, 0, ready
    )

    @pl.loop(0, out_ref.shape[1] // TILE)
    def _(tile):
        columns = pl.ds(pl.multiple_of(tile * TILE, TILE), TILE)
        out_ref[:, columns] = contract(rotated[...], tokens[:, columns], 1, 0)


def late_kernel(first_block, spans, *refs):
    count = len(spans)
    place_ref, gain_ref, ids_ref, upstream_ref, weight, before = refs[:6]
    pieces, refs = refs[6 : 6 + count], refs[6 + count :]
    out_ref, tokens, upstream, turned, rotated, sems = refs
    copies = Copies(sems)
    needed = start_upstream(copies, place_ref, first_block, upstream_ref, upstream)
    ready = start_tokens(copies, pieces, spans, tokens)
    wait_all(needed)
    rotated_gradient(
        place_ref, first_block, gain_ref, ids_ref, tokens, weight, upstream, turned, rotated, 0, ready
    )

    @pl.loop(0, out_ref.shape[1] // TILE)
    def _(tile):
        columns = pl.ds(pl.multiple_of(tile * TILE, TILE), TILE)
        out_ref[:, columns] = before[:, columns] + contract(rotated[...], tokens[:, columns], 1, 0)


def renew_kernel(first_block, count, *refs):
    place_ref, gain_ref, ids_ref, upstream_ref, weight, before_ref = refs[:6]
    refs = refs[6:]
    pieces, (theirs_ref, split, factors) = refs[:count], refs[count : count + 3]
    tokens, upstream, turned, rotated, sems = refs[count + 3 :]
    all_rows, width = weight.shape
    size = gain_ref.shape[1]
    heads = all_rows // size
    tiles = width // TILE
    copies = Copies(sems)
    needed = start_upstream(copies, place_ref, first_block, upstream_ref, upstream)
    offset = 0
    for piece in pieces:
        tokens[pl.ds(offset, piece.shape[0]), :] = piece[...]
        offset += piece.shape[0]
    wait_all(needed)
    rotated_gradient(
        place_ref, first_block, gain_ref, ids_ref, tokens, weight, upstream, turned, rotated, 0, []
    )

    @pl.loop(0, tiles)
    def _(tile):
        columns = pl.ds(pl.multiple_of(tile * TILE, TILE), TILE)
        part = contract(rotated[...], tokens[:, columns], 1, 0) + before_ref[:, columns]
        high, low = halves(part)
        for head in range(heads):
            span = slice(head * size, (head + 1) * size)
            split[head, :size, columns] = high[span]
            split[head, size:, columns] = low[span]

    grams = []
    for head in range(heads):
        both = split[head]
        whole = contract(both, both, 1, 1)
        grams.append(
            whole[:size, :size] + whole[:size, size:] + whole[size:, :size] + whole[size:, size:]
        )
    core_is_zero = place_ref[10] == 0
    for head, factor in enumerate(orthogonal_factors(grams, width)):
        for which in range(2):
            high, low = halves(rows_of_core(factor, core_is_zero, which))
            half = high.shape[0]
            factors[head, which, :half, :size] = high
            factors[head, which, :half, size:] = high
            factors[head, which, half:, :size] = low
            factors[head, which, half:, size:] = jnp.zeros_like(low)
    change_rows(place_ref, weight, split, factors, theirs_ref, 1)


def rows_of_core(value, core_is_zero, which):
    rows = []
    for begin in range(0, value.shape[0], 16):
        first, second = value[begin : begin + 8], value[begin + 8 : begin + 16]
        if which:
            first, second = second, first
        rows.append(jnp.where(core_is_zero, first, second))
    return jnp.concatenate(rows, 0)


def change_rows(place_ref, weight, split, factors, out_ref, which):
    all_rows, width = weight.shape
    heads = split.shape[0]
    size = all_rows // heads
    core_is_zero = place_ref[10] == 0
    indices = []
    for chip in range(8):
        step_y = lax.rem(chip // 2 - place_ref[8] + 4, 4)
        step_z = lax.rem(chip % 2 - place_ref[9] + 2, 2)
        indices.append(step_y * 2 + step_z)

    @pl.loop(0, width // TILE)
    def _(tile):
        columns = pl.ds(pl.multiple_of(tile * TILE, TILE), TILE)
        for pair in range(heads // 2):
            renewed = []
            for head in (2 * pair, 2 * pair + 1):
                both = contract(factors[head, which], split[head, :, columns], 1, 0)
                change = both[: size // 2] + both[size // 2 :]
                old = weight[head * size : (head + 1) * size, columns].astype(jnp.float32)
                renewed.append(rows_of_core(old, core_is_zero, which) - change)
            span = pl.ds(pair * 16, 16)
            for chip, index in enumerate(indices):
                rows = [value[chip * 8 : chip * 8 + 8] for value in renewed]
                out_ref[index, span, columns] = jnp.concatenate(rows, 0).astype(jnp.bfloat16)


def mine_kernel(place_ref, weight, split, factors, mine_ref):
    change_rows(place_ref, weight, split, factors, mine_ref, 0)


OUTSIDE = pl.BlockSpec(memory_space=pltpu.HBM)
INSIDE = pl.BlockSpec(memory_space=pltpu.VMEM)
SCALARS = pl.BlockSpec(memory_space=pltpu.SMEM)


def outside(array):
    return pltpu.with_memory_space_constraint(array, pltpu.HBM)


def call(kernel, out_shape, in_specs, out_specs, scratch, flops, moved, vmem, operands, aliases=None):
    return pl.pallas_call(
        kernel,
        out_shape=out_shape,
        in_specs=in_specs,
        out_specs=out_specs,
        scratch_shapes=scratch,
        input_output_aliases=aliases or {},
        compiler_params=pltpu.CompilerParams(vmem_limit_bytes=vmem * 1024 * 1024),
        cost_estimate=pl.CostEstimate(flops=flops, bytes_accessed=moved, transcendentals=0),
    )(*operands)


def scratch_of(common, rows):
    all_rows, width = common[-1].shape
    return [
        pltpu.VMEM((rows, all_rows), jnp.bfloat16),
        pltpu.VMEM((all_rows, rows), jnp.float32),
    ]


def arrays_of(pieces):
    return [outside(piece[0] if isinstance(piece, tuple) else piece) for piece in pieces]


def spans_of(pieces):
    return [piece[1:] if isinstance(piece, tuple) else (0, piece.shape[0]) for piece in pieces]


def rows_of(pieces):
    return sum(count for _, count in spans_of(pieces))


COMMON_SPECS = [SCALARS, INSIDE, INSIDE, OUTSIDE, INSIDE]


def pick_kernel(picks, count, *refs):
    sources, targets, sems = refs[:count], refs[-1 - len(picks) : -1], refs[-1]
    copies = Copies(sems)
    started = []
    for target, parts in zip(targets, picks):
        offset = 0
        for number, begin, rows in parts:
            source = sources[number].at[pl.ds(begin, rows)]
            started.append(copies.start(source, target.at[pl.ds(offset, rows)]))
            offset += rows
    wait_all(started)


def pick_call(arrays, picks, after=()):
    shapes = []
    for parts in picks:
        rows = sum(part[2] for part in parts)
        shapes.append(jax.ShapeDtypeStruct((rows, arrays[0].shape[1]), arrays[0].dtype))
    moved = 4 * sum(shape.size for shape in shapes)
    scratch = [pltpu.SemaphoreType.DMA((sum(len(parts) for parts in picks),))]
    return call(
        functools.partial(pick_kernel, picks, len(arrays)),
        tuple(shapes),
        [OUTSIDE] * (len(arrays) + len(after)),
        (INSIDE,) * len(shapes),
        scratch,
        0,
        moved,
        PICK_VMEM,
        [*map(outside, arrays), *after],
    )


def early_call(common, first_block, pieces):
    all_rows, width = common[-1].shape
    rows = rows_of(pieces)
    return call(
        functools.partial(early_kernel, first_block, spans_of(pieces)),
        jax.ShapeDtypeStruct((all_rows, width), jnp.float32),
        COMMON_SPECS + [OUTSIDE] * len(pieces),
        INSIDE,
        [pltpu.VMEM((rows, width), jnp.bfloat16)]
        + scratch_of(common, rows)
        + [
            pltpu.VMEM((all_rows, rows), jnp.bfloat16),
            pltpu.SemaphoreType.DMA((len(pieces) + rows // BLOCK,)),
        ],
        4 * rows * all_rows * width,
        (6 * all_rows + 2 * rows) * width,
        EARLY_VMEM,
        [*common, *arrays_of(pieces)],
    )


def late_call(common, first_block, before, pieces):
    all_rows, width = common[-1].shape
    rows = rows_of(pieces)
    return call(
        functools.partial(late_kernel, first_block, spans_of(pieces)),
        jax.ShapeDtypeStruct(before.shape, before.dtype),
        COMMON_SPECS + [INSIDE] + [OUTSIDE] * len(pieces),
        INSIDE,
        [pltpu.VMEM((rows, width), jnp.bfloat16)]
        + scratch_of(common, rows)
        + [
            pltpu.VMEM((all_rows, rows), jnp.bfloat16),
            pltpu.SemaphoreType.DMA((len(pieces) + rows // BLOCK,)),
        ],
        4 * rows * all_rows * width,
        2 * (rows + all_rows) * width,
        LATE_VMEM,
        [*common, before, *arrays_of(pieces)],
        {len(common): 0},
    )


def renew_call(common, first_block, before, pieces):
    all_rows, width = common[-1].shape
    size = common[1].shape[1]
    heads = all_rows // size
    rows = rows_of(pieces)
    shape = jax.ShapeDtypeStruct((8, all_rows // 16, width), jnp.bfloat16)
    return call(
        functools.partial(renew_kernel, first_block, len(pieces)),
        (
            shape,
            jax.ShapeDtypeStruct((heads, 2 * size, width), jnp.bfloat16),
            jax.ShapeDtypeStruct((heads, 2, size, 2 * size), jnp.bfloat16),
        ),
        COMMON_SPECS + [INSIDE] * (1 + len(pieces)),
        (INSIDE, INSIDE, INSIDE),
        [pltpu.VMEM((rows, width), jnp.bfloat16)]
        + scratch_of(common, rows)
        + [
            pltpu.VMEM((all_rows, rows), jnp.bfloat16),
            pltpu.SemaphoreType.DMA((rows // BLOCK,)),
        ],
        (4 * rows + 16 * size) * all_rows * width,
        8 * all_rows * width,
        RENEW_VMEM,
        [*common, before, *pieces],
    )


def mine_call(common, split, factors, shape):
    all_rows, width = common[-1].shape
    return call(
        mine_kernel,
        jax.ShapeDtypeStruct(shape, jnp.bfloat16),
        [SCALARS, INSIDE, INSIDE, INSIDE],
        INSIDE,
        [],
        4 * all_rows * split.shape[1] * width,
        4 * all_rows * width,
        MINE_VMEM,
        [common[0], common[-1], split, factors],
    )


def shards(
    activations,
    token_ids,
    cotangent,
    inner_weight,
    query_gain,
    outer_weight,
    momentum,
    average_weight,
):
    weights = inner_weight[0]
    head_count, head_size, model_width = weights.shape
    flat_weight = weights.reshape(head_count * head_size, model_width)

    place = lax.axis_index("grp")
    spot = lax.axis_index("rep")
    numbers = []
    for step_z, step_x in ((0, 0), (0, -1), (0, 1), (1, 0), (1, -1), (1, 1), (0, 2), (1, 2)):
        numbers.append(((place // RING + step_z) % 2) * RING + (place + step_x) % RING)
    numbers += [spot // 4, (spot // 2) % 2, spot % 2]
    common = (
        jnp.stack(numbers).astype(jnp.int32),
        query_gain[None, :],
        token_ids.reshape(2 * RING, BLOCK),
        outside(cotangent),
        flat_weight,
    )

    rows_b = BLOCK - ROWS_A
    left, right = along_x(activations, 1), along_x(activations, -1)
    own_a, own_b = pick_call([activations], [[(0, 0, ROWS_A)], [(0, ROWS_A, rows_b)]])
    over_a = across_z(own_a)
    over_left_a, over_right_a = along_x(over_a, 1), along_x(over_a, -1)
    over_b = across_z(own_b)
    left_far, right_b, sides_b = pick_call(
        [left, right],
        [
            [(0, 0, ROWS_A)],
            [(1, ROWS_A, rows_b)],
            [(0, ROWS_A, rows_b), (1, ROWS_A, rows_b)],
        ],
    )
    far_b = along_x(right_b, -1)
    far_a = along_x(left_far, 1)
    over_b2 = across_z(sides_b)
    before = early_call(common, 0, [activations, left, right, over_a, over_b])
    over_left_far, over_right_far = pick_call(
        [over_left_a, over_right_a], [[(0, 0, FAR)], [(1, FAR, ROWS_A - FAR)]], [before]
    )
    over_far0, over_far1 = along_x(over_left_far, 1), along_x(over_right_far, -1)
    over_far_b = across_z(far_b)
    late = [over_left_a, (over_b2, 0, rows_b), over_right_a, (over_b2, rows_b, rows_b)]
    before = late_call(common, 4, before, late)
    last = [far_a, far_b, over_far0, over_far1, over_far_b]
    theirs, split, factors = renew_call(common, 6, before, last)
    mine = mine_call(common, split, factors, theirs.shape)

    theirs = to_other_core(theirs)
    summed = None
    for step_y, step_z in ((2, 1), (3, 1), (1, 0), (3, 0), (0, 1), (1, 1), (2, 0), (0, 0)):
        index = step_y * 2 + step_z
        pair = mine[index].astype(jnp.float32) + theirs[index].astype(jnp.float32)
        if index:
            pair = to_chip(pair.astype(jnp.bfloat16), step_y, step_z).astype(jnp.float32)
        summed = pair if summed is None else summed + pair
    summed = summed.reshape(outer_weight.shape)

    mean_weight = summed / lax.axis_size("rep")
    pseudo = outer_weight - mean_weight
    new_momentum = 0.9 * momentum + pseudo
    new_outer = outer_weight - 0.7 * (pseudo + 0.9 * new_momentum)
    new_average = 0.9 * average_weight + 0.1 * new_outer
    return (new_outer, new_momentum, new_average)


def solution(mesh):
    placed = (
        P(("rep", "grp"), None),
        P("rep"),
        P("rep", "grp"),
        P("rep", "grp", None, None),
        P(),
        P("grp", "rep", None),
        P("grp", "rep", None),
        P("grp", "rep", None),
    )
    return jax.shard_map(
        shards,
        mesh=mesh,
        in_specs=placed,
        out_specs=(P("grp", "rep", None), P("grp", "rep", None), P("grp", "rep", None)),
        check_vma=False,
    )
```
